512 devices in a mesh: dp: 16 (over z), expert: 32 (over x, y, core).
Axes of the slice: x: 4, y: 4, z: 16, core: 2. Of those that a mesh axis runs over, the one named last changes fastest.
Arguments:
- x_rows: bfloat16 [32, 2, 4096, 2048], P('expert', None, 'dp'), may hold values from -6 to 6
- dy_rows: bfloat16 [32, 2, 4096, 768], P('expert', None, 'dp'), may hold values from -6 to 6
- counts: int32 [32, 2, 16], P('expert', None, 'dp'), may hold values from 1 to 256, as said below
- host_table: int32 [32, 2], replicated, may hold values from 0 to 31, as said below
- owned: int32 [32], replicated, may hold values from 0 to 31, each once
- master: float32 [32, 2048, 768], P('expert', 'dp'), may hold values from -6 to 6
- moment1: float32 [32, 2048, 768], P('expert', 'dp'), may hold values from -6 to 6
- moment2: float32 [32, 2048, 768], P('expert', 'dp'), may hold values from 0.25 to 4
Outputs:
- new_master: float32 [32, 2048, 768], P('expert', 'dp')
- host_weights: bfloat16 [32, 2, 2048, 768], P('expert', None, 'dp')
The draws below stay inside these ranges and needn't reach their ends.
Inputs may be any that keep to these rules, and one draw needn't show every extreme that they name: `host_table`: each expert is named by 1 to 4 host slots, never twice by one host; every expert is named. `counts`: rows past the count in a slot are padding.
All inputs are finite; a program needn't handle non-finite values.
Results may differ from the reference program's by a relative error of at most 0.0004.
Values may be sent and summed in bfloat16 or wider, within the bound.
A program may use at most 64 MiB of HBM per device.

```python
import math
import jax
import jax.numpy as jnp
from jax import lax

DW = 2048
FW = 768
SLOTS = 2
CAP = 256
ROWS = 4096
N_DP = 16
N_EXPERT = 32


def draw_host_table(key, part):
    key = jax.random.fold_in(key, 11)
    first, second = jax.random.split(key)
    order = jax.random.permutation(first, N_EXPERT).astype(jnp.int32)
    hosts = jnp.arange(N_EXPERT, dtype=jnp.int32)
    column_a = order[(hosts + 1) % N_EXPERT]
    column_b = order[hosts // 3]
    table = jnp.stack([column_a, column_b], axis=1)
    shuffle = jax.random.permutation(second, N_EXPERT)
    return table[shuffle].astype(jnp.int32)


def draw_counts(key, part):
    key = jax.random.fold_in(key, 23)
    first, second = jax.random.split(key)
    values = jax.random.randint(first, (N_EXPERT, SLOTS, N_DP), 1, CAP + 1)
    spot = jax.random.randint(second, (), 0, N_EXPERT * SLOTS * N_DP)
    flat = jnp.arange(N_EXPERT * SLOTS * N_DP, dtype=jnp.int32).reshape(N_EXPERT, SLOTS, N_DP)
    return jnp.where(flat == spot, CAP, values).astype(jnp.int32)


def levels(stream_key, shape, cuts, least, largest):
    factor_of = 1.0
    for position, blocks in cuts:
        heights = jax.random.uniform(jax.random.fold_in(jax.random.fold_in(stream_key, 6), position), (blocks,), jnp.float32, least / len(cuts), largest / len(cuts))
        factor_of = factor_of * jnp.repeat(jnp.exp(heights), shape[position] // blocks).reshape((-1,) + (1,) * (len(shape) - 1 - position))
    return factor_of


def centred(rng, shape, width, reach, cuts=(), held_as=jnp.bfloat16):
    array = jax.random.normal(rng, shape, jnp.float32) * width
    if len(cuts) > 0:
        array = levels(rng, shape, cuts, -0.22, 0.18) * array
    return jnp.clip(array, min=-reach, max=reach).astype(held_as)


def setup_inputs(seed: int = 0) -> dict:
    key_list = jax.random.split(jax.random.key(seed), 9)
    return {
        "x_rows": centred(key_list[0], (N_EXPERT, SLOTS, N_DP * CAP, DW), 1.0, 6.0, ((0, 32), (2, 16))),
        "dy_rows": centred(key_list[1], (N_EXPERT, SLOTS, N_DP * CAP, FW), 1.0, 6.0, ((0, 32), (2, 16))),
        "counts": draw_counts(jax.random.fold_in(key_list[8], 71), 0),
        "host_table": draw_host_table(jax.random.fold_in(key_list[8], 71), 0),
        "owned": jax.random.permutation(key_list[4], N_EXPERT).astype(jnp.int32),
        "master": centred(key_list[5], (N_EXPERT, DW, FW), 1.0, 6.0, ((0, 32), (1, 16)), jnp.float32),
        "moment1": centred(key_list[6], (N_EXPERT, DW, FW), 1.0, 6.0, ((0, 32), (1, 16)), jnp.float32),
        "moment2": jnp.clip(jnp.exp(math.log(4.0) - 2.7725887 * jax.random.uniform(key_list[7], (N_EXPERT, DW, FW), jnp.float32) ** levels(key_list[7], (N_EXPERT, DW, FW), ((0, 32), (1, 16)), -0.2, 0.2)), 0.25, 4.0),
    }


def reference(x_rows, dy_rows, counts, host_table, owned, master, moment1, moment2):
    hosts = x_rows.shape[0]
    slots = x_rows.shape[1]
    rows = x_rows.shape[2]
    offset = jnp.arange(rows, dtype=jnp.int32) % CAP
    shard = jnp.arange(rows, dtype=jnp.int32) // CAP

    def add_slot(total, index):
        host = index // slots
        slot = index % slots
        inputs = x_rows[host, slot].astype(jnp.float32)
        keep = offset < counts[host, slot][shard]
        grads = jnp.where(keep[:, None], dy_rows[host, slot].astype(jnp.float32), 0.0)
        term = lax.dot_general(inputs, grads, (((0,), (0,)), ((), ())), precision=lax.Precision.HIGHEST)
        return (total.at[host_table[host, slot]].add(term), None)
    start = jnp.zeros((hosts, DW, FW), jnp.float32)
    total, _ = lax.scan(add_slot, start, jnp.arange(hosts * slots, dtype=jnp.int32))
    grad = total[owned] / math.sqrt(ROWS)
    first = 0.8 * moment1 + 0.2 * grad
    second = 0.95 * moment2 + 0.05 * grad * grad
    new_master = master - 0.3 * (first / (jnp.sqrt(second) + 1e-08) + 0.1 * master)
    home = jnp.zeros((hosts,), jnp.int32).at[owned].set(jnp.arange(hosts, dtype=jnp.int32))
    host_weights = new_master[home[host_table]].astype(jnp.bfloat16)
    return (new_master, host_weights)
```

```python
import math

import jax
import jax.numpy as jnp
from jax import lax
from jax.experimental import pallas as pl
from jax.experimental.pallas import tpu as pltpu
from jax.sharding import PartitionSpec as P

N_DP = 16
N_EX = 32
SLOTS = 2
CAP = 256
BLOCK = 128
FEATS = 768
HALF = 384
PARTS = 3
LANES = 128
CODES = SLOTS * 2 * BLOCK
CHUNK = CODES + 16
TOP = 32600.0
PER_OCTAVE = 256.0
HOPS = 8
MESH = pl.DeviceIdType.MESH
FLOWS = []
for _part in range(PARTS):
    FLOWS.append((_part, 1, 8 if _part % 2 == 0 else 7))
    FLOWS.append((_part, -1, 7 if _part % 2 == 0 else 8))


def encode(values, buf):
    peaks = []
    for s in range(SLOTS):
        peak = jnp.maximum(
            jnp.max(jnp.abs(values[s][0]), axis=0), jnp.max(jnp.abs(values[s][1]), axis=0)
        )
        peaks.append(jnp.maximum(peak, 1e-20))
    level = jnp.ceil(jnp.log2(jnp.concatenate(peaks, axis=0)) * PER_OCTAVE)
    inverse = jnp.exp2(level * (-1.0 / PER_OCTAVE)) * TOP
    buf[pl.ds(CODES, 16), :] = level.astype(jnp.int32).astype(jnp.int16)
    for s in range(SLOTS):
        for c in range(2):
            scaled = values[s][c] * inverse[8 * s : 8 * s + 8][None]
            code = jnp.floor(scaled + 0.5).astype(jnp.int32).astype(jnp.int16)
            buf[pl.ds((2 * s + c) * BLOCK, BLOCK), :] = code.reshape(BLOCK, LANES)


def scales(buf):
    level = buf[pl.ds(CODES, 16), :].astype(jnp.int32).astype(jnp.float32)
    return jnp.exp2(level * (1.0 / PER_OCTAVE)) * (1.0 / TOP)


def decode(buf, scale, s, c):
    code = buf[pl.ds((2 * s + c) * BLOCK, BLOCK), :].astype(jnp.int32).astype(jnp.float32)
    return code.reshape(16, 8, LANES) * scale[8 * s : 8 * s + 8][None]


def kernel(
    x_ref, dy_ref, counts_ref, table_ref, owned_ref, master_ref, first_ref, second_ref,
    new_ref, weights_ref,
    kept, send, recv, pick, sums, slots_in, state, fresh, hosted, new_in, hosted_in,
    ring_send, ring_recv, state_send, state_recv, sums_send, sums_recv,
    new_send, new_recv, hosted_send, hosted_recv,
):
    z = lax.axis_index("dp")
    me = lax.axis_index("expert")
    my_group = me // 2
    my_half = lax.rem(me, 2)

    barrier = pltpu.get_barrier_semaphore()
    for step in (1, N_DP - 1):
        pl.semaphore_signal(
            barrier, inc=1, device_id=(lax.rem(z + step, N_DP), me), device_id_type=MESH
        )

    def greet(d, carry):
        pl.semaphore_signal(
            barrier, inc=1, device_id=(z, lax.rem(me + d, N_EX)), device_id_type=MESH
        )
        return carry

    lax.fori_loop(1, N_EX, greet, 0)

    rows = lax.broadcasted_iota(jnp.int32, (CAP, LANES), 0)
    for s in range(SLOTS):
        live = (rows < counts_ref[s]).astype(jnp.float32)
        for part in range(PARTS):
            for c in range(2):
                at = HALF * c + LANES * part
                value = dy_ref[s, :, at : at + LANES].astype(jnp.float32) * live
                kept[part, s, :, c * LANES : (c + 1) * LANES] = value.astype(jnp.bfloat16)

    def local(part, s, target):
        columns = pl.ds(pl.multiple_of(target * BLOCK, BLOCK), BLOCK)
        product = lax.dot_general(
            x_ref[s, :, columns],
            kept[part, s],
            (((0,), (0,)), ((), ())),
            preferred_element_type=jnp.float32,
        )
        return [product[:, c * LANES : (c + 1) * LANES].reshape(16, 8, LANES) for c in range(2)]

    def ring_copy(f, k):
        return pltpu.make_async_remote_copy(
            src_ref=send.at[f, k - 1],
            dst_ref=recv.at[f, k - 1],
            send_sem=ring_send.at[f, k - 1],
            recv_sem=ring_recv.at[f, k - 1],
            device_id=(lax.rem(z + FLOWS[f][1] + N_DP, N_DP), me),
            device_id_type=MESH,
        )

    def target_of(f, k):
        _, sign, hops = FLOWS[f]
        return lax.rem(z + sign * (hops + 1 - k) + N_DP, N_DP)

    for f, (part, sign, hops) in enumerate(FLOWS):
        encode([local(part, s, target_of(f, 1)) for s in range(SLOTS)], send.at[f, 0])
    pl.semaphore_wait(barrier, N_EX - 1 + 2)
    for f in range(len(FLOWS)):
        ring_copy(f, 1).start()

    arrays = (master_ref, first_ref, second_ref)

    def share_state(d, carry):
        j = lax.rem(me + d, N_EX)
        rows_of = pl.ds(pl.multiple_of(8 * (j // 2), 8), 8)
        columns_of = pl.ds(pl.multiple_of(HALF * lax.rem(j, 2), LANES), HALF)
        for a in range(3):
            pltpu.make_async_remote_copy(
                src_ref=arrays[a].at[rows_of, columns_of],
                dst_ref=state.at[a, me],
                send_sem=state_send,
                recv_sem=state_recv,
                device_id=(z, j),
                device_id_type=MESH,
            ).start()
        return carry

    lax.fori_loop(1, N_EX, share_state, 0)
    my_rows = pl.ds(pl.multiple_of(8 * my_group, 8), 8)
    for a in range(3):
        pltpu.make_async_copy(
            arrays[a].at[my_rows, pl.ds(pl.multiple_of(HALF * my_half, LANES), HALF)],
            state.at[a, me],
            state_recv,
        ).start()

    lane = lax.broadcasted_iota(jnp.int32, (16, 8 * SLOTS * N_EX), 1)
    row = lax.broadcasted_iota(jnp.int32, (16, 8 * SLOTS * N_EX), 0)

    def fill(h, names):
        for s in range(SLOTS):
            names = jnp.where(lane // 8 == h * SLOTS + s, table_ref[h, s], names)
        return names

    names = lax.fori_loop(0, N_EX, fill, jnp.zeros_like(lane))

    def fill_pick(pair, carry):
        expert = jnp.where(row < 8, owned_ref[2 * pair], owned_ref[2 * pair + 1])
        same = jnp.where((names == expert) & (lane % 8 == row % 8), 1.0, 0.0)
        pick[pl.ds(pl.multiple_of(16 * pair, 16), 16), :] = same.astype(jnp.bfloat16)
        return carry

    lax.fori_loop(0, N_EX // 2, fill_pick, 0)

    def hop(k, carry):
        for f, (part, sign, hops) in enumerate(FLOWS):

            @pl.when(k <= hops)
            def _(f=f, part=part):
                ring_copy(f, k - 1).wait_recv()
                arrived = recv.at[f, k - 2]
                scale = scales(arrived)
                values = []
                for s in range(SLOTS):
                    own = local(part, s, target_of(f, k))
                    values.append([own[c] + decode(arrived, scale, s, c) for c in range(2)])
                encode(values, send.at[f, k - 1])
                ring_copy(f, k).start()

        return carry

    lax.fori_loop(2, HOPS + 1, hop, 0)

    for part in range(PARTS):
        ends = []
        for f in (2 * part, 2 * part + 1):
            hops = FLOWS[f][2]
            ring_copy(f, hops).wait_recv()
            ends.append(recv.at[f, hops - 1])
        end_scales = [scales(end) for end in ends]
        for s in range(SLOTS):
            own = local(part, s, z)
            for c in range(2):
                value = own[c]
                for end, scale in zip(ends, end_scales):
                    value = value + decode(end, scale, s, c)
                sums[part, :, c, s] = value

        def share_sums(d, carry, part=part):
            j = lax.rem(me + d, N_EX)
            pltpu.make_async_remote_copy(
                src_ref=sums.at[part, j // 2, lax.rem(j, 2)],
                dst_ref=slots_in.at[part, me],
                send_sem=sums_send,
                recv_sem=sums_recv.at[part],
                device_id=(z, j),
                device_id_type=MESH,
            ).start()
            return carry

        lax.fori_loop(1, N_EX, share_sums, 0)
        pltpu.make_async_copy(
            sums.at[part, my_group, my_half], slots_in.at[part, me], sums_recv.at[part]
        ).start()

    pltpu.make_async_copy(state, state, state_recv).wait()
    for part in range(PARTS):
        columns = slice(LANES * part, LANES * (part + 1))
        pltpu.make_async_copy(slots_in.at[part], slots_in.at[part], sums_recv.at[part]).wait()
        value = slots_in[part].reshape(8 * SLOTS * N_EX, LANES)
        grad = jnp.zeros((8 * N_EX, LANES), jnp.float32)
        for _ in range(3):
            piece = value.astype(jnp.bfloat16)
            value = value - piece.astype(jnp.float32)
            grad = grad + jnp.dot(pick[...], piece, preferred_element_type=jnp.float32)
        grad = grad * (1.0 / math.sqrt(N_DP * CAP))
        weight = state[0, :, :, columns].reshape(8 * N_EX, LANES)
        first = 0.8 * state[1, :, :, columns].reshape(8 * N_EX, LANES) + 0.2 * grad
        second = 0.95 * state[2, :, :, columns].reshape(8 * N_EX, LANES) + 0.05 * grad * grad
        new = weight - 0.3 * (first / (jnp.sqrt(second) + 1e-08) + 0.1 * weight)
        fresh[part] = new.reshape(N_EX, 8, LANES)
        spread = lax.dot_general(
            pick[...],
            new.astype(jnp.bfloat16),
            (((0,), (0,)), ((), ())),
            preferred_element_type=jnp.float32,
        )
        hosted[part] = spread.astype(jnp.bfloat16).reshape(N_EX, 16, LANES)
        at = pl.ds(pl.multiple_of(HALF * my_half + LANES * part, LANES), LANES)

        def share_new(d, carry, part=part, at=at):
            j = lax.rem(me + d, N_EX)
            pltpu.make_async_remote_copy(
                src_ref=fresh.at[part, j],
                dst_ref=new_in.at[my_rows, at],
                send_sem=new_send,
                recv_sem=new_recv,
                device_id=(z, j),
                device_id_type=MESH,
            ).start()
            pltpu.make_async_remote_copy(
                src_ref=hosted.at[part, j],
                dst_ref=hosted_in.at[my_group, :, at],
                send_sem=hosted_send,
                recv_sem=hosted_recv,
                device_id=(z, j),
                device_id_type=MESH,
            ).start()
            return carry

        lax.fori_loop(1, N_EX, share_new, 0)
        pltpu.make_async_copy(fresh.at[part, me], new_in.at[my_rows, at], new_recv).start()
        pltpu.make_async_copy(
            hosted.at[part, me], hosted_in.at[my_group, :, at], hosted_recv
        ).start()

    pltpu.make_async_copy(new_in, new_in, new_recv).wait()
    new_ref[...] = new_in[...]
    pltpu.make_async_copy(hosted_in, hosted_in, hosted_recv).wait()
    for pair in range(8):
        both = [hosted_in[2 * pair + i].astype(jnp.float32) for i in range(2)]
        for s in range(SLOTS):
            block = jnp.concatenate([b[8 * s : 8 * s + 8] for b in both], axis=0)
            weights_ref[s, 16 * pair : 16 * pair + 16, :] = block.astype(jnp.bfloat16)

    for f, (part, sign, hops) in enumerate(FLOWS):
        for k in range(1, hops + 1):
            ring_copy(f, k).wait_send()
    sent = state.at[:, pl.ds(0, N_EX - 1)]
    pltpu.make_async_copy(sent, sent, state_send).wait()
    sent = slots_in.at[:, pl.ds(0, N_EX - 1)]
    pltpu.make_async_copy(sent, sent, sums_send).wait()
    sent = fresh.at[:, pl.ds(0, N_EX - 1)]
    pltpu.make_async_copy(sent, sent, new_send).wait()
    sent = hosted.at[:, pl.ds(0, N_EX - 1)]
    pltpu.make_async_copy(sent, sent, hosted_send).wait()


def body(x_rows, dy_rows, counts, host_table, owned, master, moment1, moment2):
    vmem = pl.BlockSpec(memory_space=pltpu.VMEM)
    smem = pl.BlockSpec(memory_space=pltpu.SMEM)
    flows = len(FLOWS)
    dma = pltpu.SemaphoreType.DMA
    new_master, host_weights = pl.pallas_call(
        kernel,
        out_shape=(
            jax.ShapeDtypeStruct((BLOCK, FEATS), jnp.float32),
            jax.ShapeDtypeStruct((SLOTS, BLOCK, FEATS), jnp.bfloat16),
        ),
        in_specs=[vmem, vmem, smem, smem, smem, vmem, vmem, vmem],
        out_specs=(vmem, vmem),
        scratch_shapes=[
            pltpu.VMEM((PARTS, SLOTS, CAP, 2 * LANES), jnp.bfloat16),
            pltpu.VMEM((flows, HOPS, CHUNK, LANES), jnp.int16),
            pltpu.VMEM((flows, HOPS, CHUNK, LANES), jnp.int16),
            pltpu.VMEM((8 * N_EX, 8 * SLOTS * N_EX), jnp.bfloat16),
            pltpu.VMEM((PARTS, 16, 2, SLOTS, 8, LANES), jnp.float32),
            pltpu.VMEM((PARTS, N_EX, SLOTS, 8, LANES), jnp.float32),
            pltpu.VMEM((3, N_EX, 8, HALF), jnp.float32),
            pltpu.VMEM((PARTS, N_EX, 8, LANES), jnp.float32),
            pltpu.VMEM((PARTS, N_EX, 16, LANES), jnp.bfloat16),
            pltpu.VMEM((BLOCK, FEATS), jnp.float32),
            pltpu.VMEM((16, 16, FEATS), jnp.bfloat16),
            dma((flows, HOPS)),
            dma((flows, HOPS)),
            dma,
            dma,
            dma,
            dma((PARTS,)),
            dma,
            dma,
            dma,
            dma,
        ],
        compiler_params=pltpu.CompilerParams(
            collective_id=0, has_side_effects=True, vmem_limit_bytes=44 * 1024 * 1024
        ),
    )(
        x_rows[0], dy_rows[0], counts.reshape(SLOTS), host_table, owned,
        master[0], moment1[0], moment2[0],
    )
    return (new_master[None], host_weights[None])


def solution(mesh):
    in_specs = (
        P("expert", None, "dp", None),
        P("expert", None, "dp", None),
        P("expert", None, "dp"),
        P(),
        P(),
        P("expert", "dp", None),
        P("expert", "dp", None),
        P("expert", "dp", None),
    )
    out_specs = (P("expert", "dp", None), P("expert", None, "dp", None))
    return jax.shard_map(body, mesh=mesh, in_specs=in_specs, out_specs=out_specs, check_vma=False)
```

```python
import math

import jax
import jax.numpy as jnp
from jax import lax
from jax.experimental import pallas as pl
from jax.experimental.pallas import tpu as pltpu
from jax.sharding import PartitionSpec as P

N_DP = 16
N_EX = 32
SLOTS = 2
CAP = 256
WIDTH = 2048
BLOCK = 128
FEATS = 768
HALF = 384
PARTS = 3
LANES = 128
LAST = 2
HOPS = 8
TOP = 32600.0
PER_OCTAVE = 256.0
MESH = pl.DeviceIdType.MESH
FLOWS = ((0, 1, 8), (0, -1, 7), (1, 1, 7), (1, -1, 8))
LAST_FLOWS = ((LAST, 1, 8), (LAST, -1, 7))
CHUNK = 4 * BLOCK + 16
LAST_CHUNK = 2 * BLOCK + 16


def level_of(peak):
    return jnp.ceil(jnp.log2(jnp.maximum(peak, 1e-20)) * PER_OCTAVE)


def to_code(value):
    return jnp.floor(value + 0.5).astype(jnp.int32).astype(jnp.int16)


def to_float(code):
    return code.astype(jnp.int32).astype(jnp.float32)


def encode(values, buf):
    count = len(values[0])
    peaks = []
    for group in values:
        peak = jnp.max(jnp.abs(group[0]), axis=0)
        for value in group[1:]:
            peak = jnp.maximum(peak, jnp.max(jnp.abs(value), axis=0))
        peaks.append(peak)
    level = level_of(jnp.concatenate(peaks, axis=0))
    inverse = jnp.exp2(level * (-1.0 / PER_OCTAVE)) * TOP
    buf[pl.ds(2 * count * BLOCK, 16), :] = level.astype(jnp.int32).astype(jnp.int16)
    for s, group in enumerate(values):
        for c, value in enumerate(group):
            code = to_code(value * inverse[8 * s : 8 * s + 8][None])
            buf[pl.ds((count * s + c) * BLOCK, BLOCK), :] = code.reshape(BLOCK, LANES)


def scale_of(level):
    return jnp.exp2(to_float(level) * (1.0 / PER_OCTAVE)) * (1.0 / TOP)


def decode(buf, scale, count, s, c):
    code = to_float(buf[pl.ds((count * s + c) * BLOCK, BLOCK), :])
    return code.reshape(16, 8, LANES) * scale[8 * s : 8 * s + 8][None]


def kernel(
    x_hbm, dy_hbm, counts_hbm, table_hbm, owned_hbm, master_hbm, first_hbm, second_hbm,
    new_ref, weights_ref,
    x_ref, dy_ref, counts_ref, table_ref, owned_ref, mine,
    kept, send, recv, last_send, last_recv, last_own,
    early, early_inverse, level_out, level_in, early_scale, code_out, code_in,
    pick, sums, slots_in, state, fresh, hosted, new_in, hosted_in,
    load_sem, ring_send, ring_recv, last_ring_send, last_ring_recv,
    level_send, level_recv, code_send, code_recv, state_send, state_recv,
    sums_send, sums_recv, new_send, new_recv, hosted_send, hosted_recv,
):
    z = lax.axis_index("dp")
    me = lax.axis_index("expert")
    my_group = me // 2
    my_half = lax.rem(me, 2)

    loads = [
        pltpu.make_async_copy(src, dst, load_sem.at[i])
        for i, (src, dst) in enumerate(
            (
                (counts_hbm, counts_ref),
                (dy_hbm, dy_ref),
                (x_hbm, x_ref),
                (table_hbm, table_ref),
                (owned_hbm, owned_ref),
                (master_hbm, mine.at[0]),
                (first_hbm, mine.at[1]),
                (second_hbm, mine.at[2]),
            )
        )
    ]
    for load in loads:
        load.start()

    barrier = pltpu.get_barrier_semaphore()
    for step in (1, N_DP - 1):
        pl.semaphore_signal(
            barrier, inc=1, device_id=(lax.rem(z + step, N_DP), me), device_id_type=MESH
        )

    def greet(d, carry):
        pl.semaphore_signal(
            barrier, inc=1, device_id=(z, lax.rem(me + d, N_EX)), device_id_type=MESH
        )
        return carry

    lax.fori_loop(1, N_EX, greet, 0)

    loads[0].wait()
    loads[1].wait()
    rows = lax.broadcasted_iota(jnp.int32, (CAP, LANES), 0)
    for s in range(SLOTS):
        live = (rows < counts_ref[s]).astype(jnp.float32)
        for part in range(PARTS):
            for c in range(2):
                at = HALF * c + LANES * part
                value = dy_ref[s, :, at : at + LANES].astype(jnp.float32) * live
                kept[part, s, :, c * LANES : (c + 1) * LANES] = value.astype(jnp.bfloat16)
    loads[2].wait()

    def local(part, s, target):
        columns = pl.ds(pl.multiple_of(target * BLOCK, BLOCK), BLOCK)
        product = lax.dot_general(
            x_ref[s, :, columns],
            kept[part, s],
            (((0,), (0,)), ((), ())),
            preferred_element_type=jnp.float32,
        )
        return [product[:, c * LANES : (c + 1) * LANES].reshape(16, 8, LANES) for c in range(2)]

    def neighbour(sign):
        return (lax.rem(z + sign + N_DP, N_DP), me)

    def target_of(flow, k):
        _, sign, hops = flow
        return lax.rem(z + sign * (hops + 1 - k) + N_DP, N_DP)

    def ring_copy(f, k):
        return pltpu.make_async_remote_copy(
            src_ref=send.at[f, k - 1],
            dst_ref=recv.at[f, k - 1],
            send_sem=ring_send.at[f, k - 1],
            recv_sem=ring_recv.at[f, k - 1],
            device_id=neighbour(FLOWS[f][1]),
            device_id_type=MESH,
        )

    def last_copy(f, k):
        return pltpu.make_async_remote_copy(
            src_ref=last_send.at[f, k - 1],
            dst_ref=last_recv.at[f, k - 1],
            send_sem=last_ring_send.at[f, k - 1],
            recv_sem=last_ring_recv.at[f, k - 1],
            device_id=neighbour(LAST_FLOWS[f][1]),
            device_id_type=MESH,
        )

    for f, flow in enumerate(FLOWS):
        encode([local(flow[0], s, target_of(flow, 1)) for s in range(SLOTS)], send.at[f, 0])
    pl.semaphore_wait(barrier, N_EX - 1 + 2)
    for f in range(len(FLOWS)):
        ring_copy(f, 1).start()

    for s in range(SLOTS):
        for c in range(2):
            early_inverse[s, c] = jnp.zeros((16, 8, LANES), jnp.float32)

    def multiply(k, carry):
        for i, flow in enumerate(LAST_FLOWS):
            for s in range(SLOTS):
                products = local(LAST, s, target_of(flow, k))
                for c in range(2):
                    early[2 * (k - 1) + i, s, c] = products[c]
                    early_inverse[s, c] = jnp.maximum(early_inverse[s, c], jnp.abs(products[c]))
        return carry

    lax.fori_loop(1, HOPS + 1, multiply, 0)
    for c in range(2):
        levels = []
        for s in range(SLOTS):
            level = level_of(early_inverse[s, c])
            early_inverse[s, c] = jnp.exp2(level * (-1.0 / PER_OCTAVE)) * TOP
            levels.append(level)
        level_out[:, c] = jnp.concatenate(levels, axis=1).astype(jnp.int32).astype(jnp.int16)

    def share_levels(d, carry):
        j = lax.rem(me + d, N_EX)
        pltpu.make_async_remote_copy(
            src_ref=level_out.at[j // 2, lax.rem(j, 2)],
            dst_ref=level_in.at[me],
            send_sem=level_send,
            recv_sem=level_recv,
            device_id=(z, j),
            device_id_type=MESH,
        ).start()
        return carry

    lax.fori_loop(1, N_EX, share_levels, 0)
    pltpu.make_async_copy(level_out.at[my_group, my_half], level_in.at[me], level_recv).start()

    def spread_codes(k):
        both = pl.ds(2 * (k - 1), 2)
        for i in range(2):
            o = 2 * (k - 1) + i
            for c in range(2):
                codes = [
                    jnp.floor(early[o, s, c] * early_inverse[s, c] + 0.5) for s in range(SLOTS)
                ]
                code = jnp.concatenate(codes, axis=1).astype(jnp.int32).astype(jnp.int16)
                code_out[:, c, o] = code

        def share_codes(d, carry):
            j = lax.rem(me + d, N_EX)
            pltpu.make_async_remote_copy(
                src_ref=code_out.at[j // 2, lax.rem(j, 2), both],
                dst_ref=code_in.at[me, both],
                send_sem=code_send,
                recv_sem=code_recv.at[k - 1],
                device_id=(z, j),
                device_id_type=MESH,
            ).start()
            return carry

        lax.fori_loop(1, N_EX, share_codes, 0)
        pltpu.make_async_copy(
            code_out.at[my_group, my_half, both], code_in.at[me, both], code_recv.at[k - 1]
        ).start()

    def share_state(d, carry):
        j = lax.rem(me + d, N_EX)
        rows_of = pl.ds(pl.multiple_of(8 * (j // 2), 8), 8)
        columns_of = pl.ds(pl.multiple_of(HALF * lax.rem(j, 2), LANES), HALF)
        for a in range(3):
            pltpu.make_async_remote_copy(
                src_ref=mine.at[a, rows_of, columns_of],
                dst_ref=state.at[a, me],
                send_sem=state_send,
                recv_sem=state_recv,
                device_id=(z, j),
                device_id_type=MESH,
            ).start()
        return carry

    def merge_early(k):
        both = pl.ds(2 * (k - 1), 2)
        arrived = code_in.at[:, both]
        pltpu.make_async_copy(arrived, arrived, code_recv.at[k - 1]).wait()
        high = []
        low = []
        for i in range(2):
            value = to_float(code_in[:, 2 * (k - 1) + i]) * early_scale[...]
            value = value.reshape(8 * SLOTS * N_EX, LANES)
            top = value.astype(jnp.bfloat16)
            high.append(top)
            low.append((value - top.astype(jnp.float32)).astype(jnp.bfloat16))
        merged = jnp.dot(
            pick[...], jnp.concatenate(high, axis=1), preferred_element_type=jnp.float32
        ) + jnp.dot(pick[...], jnp.concatenate(low, axis=1), preferred_element_type=jnp.float32)
        return [merged[:, i * LANES : (i + 1) * LANES].reshape(2, 16, 8, LANES) for i in range(2)]

    def last_arrived(f, k):
        last_copy(f, k).wait_recv()
        buf = last_recv.at[f, k - 1]
        scale = scale_of(buf[pl.ds(2 * BLOCK, 16), :])
        return [decode(buf, scale, 1, g, 0) for g in range(2)]

    spread_codes(1)

    for load in loads[3:]:
        load.wait()
    lane = lax.broadcasted_iota(jnp.int32, (16, 8 * SLOTS * N_EX), 1)
    row = lax.broadcasted_iota(jnp.int32, (16, 8 * SLOTS * N_EX), 0)

    def fill(h, names):
        for s in range(SLOTS):
            names = jnp.where(lane // 8 == h * SLOTS + s, table_ref[s, h], names)
        return names

    names = lax.fori_loop(0, N_EX, fill, jnp.zeros_like(lane))

    def fill_pick(pair, carry):
        expert = jnp.where(row < 8, owned_ref[2 * pair], owned_ref[2 * pair + 1])
        same = jnp.where((names == expert) & (lane % 8 == row % 8), 1.0, 0.0)
        pick[pl.ds(pl.multiple_of(16 * pair, 16), 16), :] = same.astype(jnp.bfloat16)
        return carry

    lax.fori_loop(0, N_EX // 2, fill_pick, 0)

    spread_codes(2)
    lax.fori_loop(1, 5, share_state, 0)
    for a in range(3):
        pltpu.make_async_copy(
            mine.at[
                a,
                pl.ds(pl.multiple_of(8 * my_group, 8), 8),
                pl.ds(pl.multiple_of(HALF * my_half, LANES), HALF),
            ],
            state.at[a, me],
            state_recv,
        ).start()
    pltpu.make_async_copy(level_in, level_in, level_recv).wait()
    early_scale[...] = scale_of(level_in[...])
    merged = merge_early(1)
    for f in range(2):
        encode([[merged[f][g]] for g in range(2)], last_send.at[f, 0])
        last_copy(f, 1).start()

    def hop(k, carry):
        for f, flow in enumerate(FLOWS):

            @pl.when(k <= flow[2])
            def _(f=f, flow=flow):
                ring_copy(f, k - 1).wait_recv()
                arrived = recv.at[f, k - 2]
                scale = scale_of(arrived[pl.ds(4 * BLOCK, 16), :])
                values = []
                for s in range(SLOTS):
                    own = local(flow[0], s, target_of(flow, k))
                    values.append([own[c] + decode(arrived, scale, 2, s, c) for c in range(2)])
                encode(values, send.at[f, k - 1])
                ring_copy(f, k).start()

        @pl.when(k < HOPS)
        def _():
            spread_codes(k + 1)

        lax.fori_loop(4 * k - 3, jnp.minimum(4 * k + 1, N_EX), share_state, 0)

        merged = merge_early(k)
        arrived = last_arrived(0, k - 1)
        encode([[merged[0][g] + arrived[g]] for g in range(2)], last_send.at[0, k - 1])
        last_copy(0, k).start()

        @pl.when(k < HOPS)
        def _():
            arrived = last_arrived(1, k - 1)
            encode([[merged[1][g] + arrived[g]] for g in range(2)], last_send.at[1, k - 1])
            last_copy(1, k).start()

        @pl.when(k == HOPS)
        def _():
            last_own[...] = merged[1]

        return carry

    lax.fori_loop(2, HOPS + 1, hop, 0)

    for part in range(LAST):
        ends = []
        for f in (2 * part, 2 * part + 1):
            hops = FLOWS[f][2]
            ring_copy(f, hops).wait_recv()
            ends.append(recv.at[f, hops - 1])
        end_scales = [scale_of(end[pl.ds(4 * BLOCK, 16), :]) for end in ends]
        for s in range(SLOTS):
            own = local(part, s, z)
            for c in range(2):
                value = own[c]
                for end, scale in zip(ends, end_scales):
                    value = value + decode(end, scale, 2, s, c)
                sums[part, :, c, s] = value

        def share_sums(d, carry, part=part):
            j = lax.rem(me + d, N_EX)
            pltpu.make_async_remote_copy(
                src_ref=sums.at[part, j // 2, lax.rem(j, 2)],
                dst_ref=slots_in.at[part, me],
                send_sem=sums_send,
                recv_sem=sums_recv.at[part],
                device_id=(z, j),
                device_id_type=MESH,
            ).start()
            return carry

        lax.fori_loop(1, N_EX, share_sums, 0)
        pltpu.make_async_copy(
            sums.at[part, my_group, my_half], slots_in.at[part, me], sums_recv.at[part]
        ).start()

    my_rows = pl.ds(pl.multiple_of(8 * my_group, 8), 8)

    def apply(part, total):
        columns = slice(LANES * part, LANES * (part + 1))
        grad = total * (1.0 / math.sqrt(N_DP * CAP))
        weight = state[0, :, :, columns].reshape(8 * N_EX, LANES)
        first = 0.8 * state[1, :, :, columns].reshape(8 * N_EX, LANES) + 0.2 * grad
        second = 0.95 * state[2, :, :, columns].reshape(8 * N_EX, LANES) + 0.05 * grad * grad
        new = weight - 0.3 * (first / (jnp.sqrt(second) + 1e-08) + 0.1 * weight)
        fresh[part] = new.reshape(N_EX, 8, LANES)
        spread = lax.dot_general(
            pick[...],
            new.astype(jnp.bfloat16),
            (((0,), (0,)), ((), ())),
            preferred_element_type=jnp.float32,
        )
        hosted[part] = spread.astype(jnp.bfloat16).reshape(N_EX, 16, LANES)
        at = pl.ds(pl.multiple_of(HALF * my_half + LANES * part, LANES), LANES)

        def share_new(d, carry):
            j = lax.rem(me + d, N_EX)
            pltpu.make_async_remote_copy(
                src_ref=fresh.at[part, j],
                dst_ref=new_in.at[my_rows, at],
                send_sem=new_send,
                recv_sem=new_recv,
                device_id=(z, j),
                device_id_type=MESH,
            ).start()
            pltpu.make_async_remote_copy(
                src_ref=hosted.at[part, j],
                dst_ref=hosted_in.at[my_group, :, at],
                send_sem=hosted_send,
                recv_sem=hosted_recv,
                device_id=(z, j),
                device_id_type=MESH,
            ).start()
            return carry

        lax.fori_loop(1, N_EX, share_new, 0)
        pltpu.make_async_copy(fresh.at[part, me], new_in.at[my_rows, at], new_recv).start()
        pltpu.make_async_copy(
            hosted.at[part, me], hosted_in.at[my_group, :, at], hosted_recv
        ).start()

    pltpu.make_async_copy(state, state, state_recv).wait()
    up = last_arrived(0, LAST_FLOWS[0][2])
    down = last_arrived(1, LAST_FLOWS[1][2])
    total = jnp.concatenate(
        [(last_own[g] + up[g] + down[g]).reshape(BLOCK, LANES) for g in range(2)], axis=0
    )
    apply(LAST, total)

    for part in range(LAST):
        pltpu.make_async_copy(slots_in.at[part], slots_in.at[part], sums_recv.at[part]).wait()
        value = slots_in[part].reshape(8 * SLOTS * N_EX, LANES)
        total = jnp.zeros((8 * N_EX, LANES), jnp.float32)
        for _ in range(3):
            piece = value.astype(jnp.bfloat16)
            value = value - piece.astype(jnp.float32)
            total = total + jnp.dot(pick[...], piece, preferred_element_type=jnp.float32)
        apply(part, total)

    pltpu.make_async_copy(new_in, new_in, new_recv).wait()
    new_ref[...] = new_in[...]
    pltpu.make_async_copy(hosted_in, hosted_in, hosted_recv).wait()
    for pair in range(8):
        both = [hosted_in[2 * pair + i].astype(jnp.float32) for i in range(2)]
        for s in range(SLOTS):
            block = jnp.concatenate([b[8 * s : 8 * s + 8] for b in both], axis=0)
            weights_ref[s, 16 * pair : 16 * pair + 16, :] = block.astype(jnp.bfloat16)

    for f, flow in enumerate(FLOWS):
        for k in range(1, flow[2] + 1):
            ring_copy(f, k).wait_send()
    for f, flow in enumerate(LAST_FLOWS):
        for k in range(1, flow[2] + 1):
            last_copy(f, k).wait_send()
    others = pl.ds(0, N_EX - 1)
    for sent, sem in (
        (level_in.at[others], level_send),
        (code_in.at[others], code_send),
        (state.at[:, others], state_send),
        (slots_in.at[:, others], sums_send),
        (fresh.at[:, others], new_send),
        (hosted.at[:, others], hosted_send),
    ):
        pltpu.make_async_copy(sent, sent, sem).wait()


def body(x_rows, dy_rows, counts, host_table, owned, master, moment1, moment2):
    vmem = pl.BlockSpec(memory_space=pltpu.VMEM)
    hbm = pl.BlockSpec(memory_space=pltpu.HBM)
    dma = pltpu.SemaphoreType.DMA
    flows = len(FLOWS)
    new_master, host_weights = pl.pallas_call(
        kernel,
        out_shape=(
            jax.ShapeDtypeStruct((BLOCK, FEATS), jnp.float32),
            jax.ShapeDtypeStruct((SLOTS, BLOCK, FEATS), jnp.bfloat16),
        ),
        in_specs=[hbm] * 8,
        out_specs=(vmem, vmem),
        scratch_shapes=[
            pltpu.VMEM((SLOTS, CAP, WIDTH), jnp.bfloat16),
            pltpu.VMEM((SLOTS, CAP, FEATS), jnp.bfloat16),
            pltpu.SMEM((SLOTS,), jnp.int32),
            pltpu.SMEM((SLOTS, N_EX), jnp.int32),
            pltpu.SMEM((N_EX,), jnp.int32),
            pltpu.VMEM((3, BLOCK, FEATS), jnp.float32),
            pltpu.VMEM((PARTS, SLOTS, CAP, 2 * LANES), jnp.bfloat16),
            pltpu.VMEM((flows, HOPS, CHUNK, LANES), jnp.int16),
            pltpu.VMEM((flows, HOPS, CHUNK, LANES), jnp.int16),
            pltpu.VMEM((2, HOPS, LAST_CHUNK, LANES), jnp.int16),
            pltpu.VMEM((2, HOPS, LAST_CHUNK, LANES), jnp.int16),
            pltpu.VMEM((2, 16, 8, LANES), jnp.float32),
            pltpu.VMEM((2 * HOPS, SLOTS, 2, 16, 8, LANES), jnp.float32),
            pltpu.VMEM((SLOTS, 2, 16, 8, LANES), jnp.float32),
            pltpu.VMEM((16, 2, 16, LANES), jnp.int16),
            pltpu.VMEM((N_EX, 16, LANES), jnp.int16),
            pltpu.VMEM((N_EX, 16, LANES), jnp.float32),
            pltpu.VMEM((16, 2, 2 * HOPS, 16, LANES), jnp.int16),
            pltpu.VMEM((N_EX, 2 * HOPS, 16, LANES), jnp.int16),
            pltpu.VMEM((8 * N_EX, 8 * SLOTS * N_EX), jnp.bfloat16),
            pltpu.VMEM((LAST, 16, 2, SLOTS, 8, LANES), jnp.float32),
            pltpu.VMEM((LAST, N_EX, SLOTS, 8, LANES), jnp.float32),
            pltpu.VMEM((3, N_EX, 8, HALF), jnp.float32),
            pltpu.VMEM((PARTS, N_EX, 8, LANES), jnp.float32),
            pltpu.VMEM((PARTS, N_EX, 16, LANES), jnp.bfloat16),
            pltpu.VMEM((BLOCK, FEATS), jnp.float32),
            pltpu.VMEM((16, 16, FEATS), jnp.bfloat16),
            dma((8,)),
            dma((flows, HOPS)),
            dma((flows, HOPS)),
            dma((2, HOPS)),
            dma((2, HOPS)),
            dma,
            dma,
            dma,
            dma((HOPS,)),
            dma,
            dma,
            dma,
            dma((LAST,)),
            dma,
            dma,
            dma,
            dma,
        ],
        compiler_params=pltpu.CompilerParams(
            collective_id=0, has_side_effects=True, vmem_limit_bytes=62 * 1024 * 1024
        ),
    )(
        x_rows[0], dy_rows[0], counts.reshape(SLOTS), host_table.T, owned,
        master[0], moment1[0], moment2[0],
    )
    return (new_master[None], host_weights[None])


def solution(mesh):
    in_specs = (
        P("expert", None, "dp", None),
        P("expert", None, "dp", None),
        P("expert", None, "dp"),
        P(),
        P(),
        P("expert", "dp", None),
        P("expert", "dp", None),
        P("expert", "dp", None),
    )
    out_specs = (P("expert", "dp", None), P("expert", None, "dp", None))
    return jax.shard_map(body, mesh=mesh, in_specs=in_specs, out_specs=out_specs, check_vma=False)
```

```python
import math

import jax
import jax.numpy as jnp
from jax import lax
from jax.experimental import pallas as pl
from jax.experimental.pallas import tpu as pltpu
from jax.sharding import PartitionSpec as P

N_DP = 16
N_EX = 32
SLOTS = 2
CAP = 256
WIDTH = 2048
BLOCK = 128
FEATS = 768
HALF = 384
PARTS = 3
LANES = 128
LAST = 2
HOPS = 8
LAG = 3
TOP = 32600.0
PER_OCTAVE = 256.0
MESH = pl.DeviceIdType.MESH
FLOWS = ((0, 1, 8), (0, -1, 7), (1, 1, 7), (1, -1, 8))
LAST_FLOWS = ((LAST, 1, 8), (LAST, -1, 7))
CHUNK = 4 * BLOCK + 16
LAST_CHUNK = 2 * BLOCK + 16


def level_of(peak):
    return jnp.ceil(jnp.log2(jnp.maximum(peak, 1e-20)) * PER_OCTAVE)


def to_code(value):
    return jnp.floor(value + 0.5).astype(jnp.int32).astype(jnp.int16)


def to_float(code):
    return code.astype(jnp.int32).astype(jnp.float32)


def encode(values, buf):
    count = len(values[0])
    peaks = []
    for group in values:
        peak = jnp.max(jnp.abs(group[0]), axis=0)
        for value in group[1:]:
            peak = jnp.maximum(peak, jnp.max(jnp.abs(value), axis=0))
        peaks.append(peak)
    level = level_of(jnp.concatenate(peaks, axis=0))
    inverse = jnp.exp2(level * (-1.0 / PER_OCTAVE)) * TOP
    buf[pl.ds(2 * count * BLOCK, 16), :] = level.astype(jnp.int32).astype(jnp.int16)
    for s, group in enumerate(values):
        for c, value in enumerate(group):
            code = to_code(value * inverse[8 * s : 8 * s + 8][None])
            buf[pl.ds((count * s + c) * BLOCK, BLOCK), :] = code.reshape(BLOCK, LANES)


def scale_of(level):
    return jnp.exp2(to_float(level) * (1.0 / PER_OCTAVE)) * (1.0 / TOP)


def decode(buf, scale, count, s, c):
    code = to_float(buf[pl.ds((count * s + c) * BLOCK, BLOCK), :])
    return code.reshape(16, 8, LANES) * scale[8 * s : 8 * s + 8][None]


def kernel(
    x_hbm, dy_hbm, counts_hbm, table_hbm, owned_hbm, master_hbm, first_hbm, second_hbm,
    new_in, hosted_in,
    x_ref, dy_ref, counts_ref, table_ref, owned_ref, mine,
    kept, send, recv, last_send, last_recv, last_own,
    early, early_inverse, level_out, level_in, early_scale, code_out, code_in,
    pick, sums, slots_in, state, fresh, hosted,
    load_sem, ring_send, ring_recv, last_ring_send, last_ring_recv,
    level_send, level_recv, code_send, code_recv, state_send, state_recv,
    sums_send, sums_recv, new_send, new_recv, hosted_send, hosted_recv,
):
    z = lax.axis_index("dp")
    me = lax.axis_index("expert")
    my_group = me // 2
    my_half = lax.rem(me, 2)

    loads = [
        pltpu.make_async_copy(src, dst, load_sem.at[i])
        for i, (src, dst) in enumerate(
            (
                (counts_hbm, counts_ref),
                (dy_hbm, dy_ref),
                (x_hbm, x_ref),
                (table_hbm, table_ref),
                (owned_hbm, owned_ref),
                (master_hbm, mine.at[0]),
                (first_hbm, mine.at[1]),
                (second_hbm, mine.at[2]),
            )
        )
    ]
    for load in loads:
        load.start()

    barrier = pltpu.get_barrier_semaphore()
    for step in (1, N_DP - 1):
        pl.semaphore_signal(
            barrier, inc=1, device_id=(lax.rem(z + step, N_DP), me), device_id_type=MESH
        )

    def greet(d, carry):
        pl.semaphore_signal(
            barrier, inc=1, device_id=(z, lax.rem(me + d, N_EX)), device_id_type=MESH
        )
        return carry

    lax.fori_loop(1, N_EX, greet, 0)

    def keep(part):
        rows = lax.broadcasted_iota(jnp.int32, (CAP, LANES), 0)
        for s in range(SLOTS):
            live = (rows < counts_ref[s]).astype(jnp.float32)
            for c in range(2):
                at = HALF * c + LANES * part
                value = dy_ref[s, :, at : at + LANES].astype(jnp.float32) * live
                kept[part, s, :, c * LANES : (c + 1) * LANES] = value.astype(jnp.bfloat16)

    def local(part, s, target):
        columns = pl.ds(pl.multiple_of(target * BLOCK, BLOCK), BLOCK)
        product = lax.dot_general(
            x_ref[s, :, columns],
            kept[part, s],
            (((0,), (0,)), ((), ())),
            preferred_element_type=jnp.float32,
        )
        return [product[:, c * LANES : (c + 1) * LANES].reshape(16, 8, LANES) for c in range(2)]

    def neighbour(sign):
        return (lax.rem(z + sign + N_DP, N_DP), me)

    def target_of(flow, k):
        _, sign, hops = flow
        return lax.rem(z + sign * (hops + 1 - k) + N_DP, N_DP)

    def ring_copy(f, k):
        return pltpu.make_async_remote_copy(
            src_ref=send.at[f, k - 1],
            dst_ref=recv.at[f, k - 1],
            send_sem=ring_send.at[f, k - 1],
            recv_sem=ring_recv.at[f, k - 1],
            device_id=neighbour(FLOWS[f][1]),
            device_id_type=MESH,
        )

    def last_copy(f, k):
        return pltpu.make_async_remote_copy(
            src_ref=last_send.at[f, k - 1],
            dst_ref=last_recv.at[f, k],
            send_sem=last_ring_send.at[f, k - 1],
            recv_sem=last_ring_recv.at[f, k - 1],
            device_id=neighbour(LAST_FLOWS[f][1]),
            device_id_type=MESH,
        )

    for load in loads[:3]:
        load.wait()
    for f, flow in enumerate(FLOWS):
        if f % 2 == 0:
            keep(flow[0])
        encode([local(flow[0], s, target_of(flow, 1)) for s in range(SLOTS)], send.at[f, 0])
        if f == 0:
            pl.semaphore_wait(barrier, N_EX - 1 + 2)
        ring_copy(f, 1).start()
    keep(LAST)

    for s in range(SLOTS):
        for c in range(2):
            early_inverse[s, c] = jnp.zeros((16, 8, LANES), jnp.float32)

    def multiply(k, carry):
        for i, flow in enumerate(LAST_FLOWS):
            for s in range(SLOTS):
                products = local(LAST, s, target_of(flow, k))
                for c in range(2):
                    early[2 * (k - 1) + i, s, c] = products[c]
                    early_inverse[s, c] = jnp.maximum(early_inverse[s, c], jnp.abs(products[c]))
        return carry

    lax.fori_loop(1, HOPS + 1, multiply, 0)
    for c in range(2):
        levels = []
        for s in range(SLOTS):
            level = level_of(early_inverse[s, c])
            early_inverse[s, c] = jnp.exp2(level * (-1.0 / PER_OCTAVE)) * TOP
            levels.append(level)
        level_out[:, c] = jnp.concatenate(levels, axis=1).astype(jnp.int32).astype(jnp.int16)

    def share_levels(d, carry):
        j = lax.rem(me + d, N_EX)
        pltpu.make_async_remote_copy(
            src_ref=level_out.at[j // 2, lax.rem(j, 2)],
            dst_ref=level_in.at[me],
            send_sem=level_send,
            recv_sem=level_recv,
            device_id=(z, j),
            device_id_type=MESH,
        ).start()
        return carry

    lax.fori_loop(1, N_EX, share_levels, 0)
    pltpu.make_async_copy(level_out.at[my_group, my_half], level_in.at[me], level_recv).start()

    def spread_codes(k):
        both = pl.ds(2 * (k - 1), 2)
        for i in range(2):
            o = 2 * (k - 1) + i
            for c in range(2):
                codes = [
                    jnp.floor(early[o, s, c] * early_inverse[s, c] + 0.5) for s in range(SLOTS)
                ]
                code = jnp.concatenate(codes, axis=1).astype(jnp.int32).astype(jnp.int16)
                code_out[:, c, o] = code

        def share_codes(d, carry):
            j = lax.rem(me + d, N_EX)
            pltpu.make_async_remote_copy(
                src_ref=code_out.at[j // 2, lax.rem(j, 2), both],
                dst_ref=code_in.at[me, both],
                send_sem=code_send,
                recv_sem=code_recv.at[k - 1],
                device_id=(z, j),
                device_id_type=MESH,
            ).start()
            return carry

        lax.fori_loop(1, N_EX, share_codes, 0)
        pltpu.make_async_copy(
            code_out.at[my_group, my_half, both], code_in.at[me, both], code_recv.at[k - 1]
        ).start()

    def share_state(d, carry):
        j = lax.rem(me + d, N_EX)
        rows_of = pl.ds(pl.multiple_of(8 * (j // 2), 8), 8)
        columns_of = pl.ds(pl.multiple_of(HALF * lax.rem(j, 2), LANES), HALF)
        for a in range(3):
            pltpu.make_async_remote_copy(
                src_ref=mine.at[a, rows_of, columns_of],
                dst_ref=state.at[a, me],
                send_sem=state_send,
                recv_sem=state_recv,
                device_id=(z, j),
                device_id_type=MESH,
            ).start()
        return carry

    def merge_early(k):
        both = pl.ds(2 * (k - 1), 2)
        arrived = code_in.at[:, both]
        pltpu.make_async_copy(arrived, arrived, code_recv.at[k - 1]).wait()
        high = []
        low = []
        for i in range(2):
            value = to_float(code_in[:, 2 * (k - 1) + i]) * early_scale[...]
            value = value.reshape(8 * SLOTS * N_EX, LANES)
            top = value.astype(jnp.bfloat16)
            high.append(top)
            low.append((value - top.astype(jnp.float32)).astype(jnp.bfloat16))
        merged = jnp.dot(
            pick[...], jnp.concatenate(high, axis=1), preferred_element_type=jnp.float32
        ) + jnp.dot(pick[...], jnp.concatenate(low, axis=1), preferred_element_type=jnp.float32)
        return [merged[:, i * LANES : (i + 1) * LANES].reshape(2, 16, 8, LANES) for i in range(2)]

    def last_arrived(f, k):
        buf = last_recv.at[f, k]
        scale = scale_of(buf[pl.ds(2 * BLOCK, 16), :])
        return [decode(buf, scale, 1, g, 0) for g in range(2)]

    def last_step(k):
        merged = merge_early(k)

        @pl.when(k > 1)
        def _():
            last_copy(0, k - 1).wait_recv()

        arrived = last_arrived(0, k - 1)
        encode([[merged[0][g] + arrived[g]] for g in range(2)], last_send.at[0, k - 1])
        last_copy(0, k).start()

        @pl.when(k > 1)
        def _():
            last_copy(1, k - 1).wait_recv()

        arrived = last_arrived(1, k - 1)
        values = [merged[1][g] + arrived[g] for g in range(2)]

        @pl.when(k < HOPS)
        def _():
            encode([[value] for value in values], last_send.at[1, k - 1])
            last_copy(1, k).start()

        @pl.when(k == HOPS)
        def _():
            for g in range(2):
                last_own[g] = values[g]

    last_recv[:, 0] = jnp.zeros((2, LAST_CHUNK, LANES), jnp.int16)
    spread_codes(1)

    for load in loads[3:]:
        load.wait()
    lane = lax.broadcasted_iota(jnp.int32, (16, 8 * SLOTS * N_EX), 1)
    row = lax.broadcasted_iota(jnp.int32, (16, 8 * SLOTS * N_EX), 0)

    def fill(h, names):
        for s in range(SLOTS):
            names = jnp.where(lane // 8 == h * SLOTS + s, table_ref[s, h], names)
        return names

    names = lax.fori_loop(0, N_EX, fill, jnp.zeros_like(lane))

    def fill_pick(pair, carry):
        expert = jnp.where(row < 8, owned_ref[2 * pair], owned_ref[2 * pair + 1])
        same = jnp.where((names == expert) & (lane % 8 == row % 8), 1.0, 0.0)
        pick[pl.ds(pl.multiple_of(16 * pair, 16), 16), :] = same.astype(jnp.bfloat16)
        return carry

    lax.fori_loop(0, N_EX // 2, fill_pick, 0)

    lax.fori_loop(1, 5, share_state, 0)
    for a in range(3):
        pltpu.make_async_copy(
            mine.at[
                a,
                pl.ds(pl.multiple_of(8 * my_group, 8), 8),
                pl.ds(pl.multiple_of(HALF * my_half, LANES), HALF),
            ],
            state.at[a, me],
            state_recv,
        ).start()
    pltpu.make_async_copy(level_in, level_in, level_recv).wait()
    early_scale[...] = scale_of(level_in[...])
    def hop(k, carry):
        for f, flow in enumerate(FLOWS):

            @pl.when(k <= flow[2])
            def _(f=f, flow=flow):
                ring_copy(f, k - 1).wait_recv()
                arrived = recv.at[f, k - 2]
                scale = scale_of(arrived[pl.ds(4 * BLOCK, 16), :])
                values = []
                for s in range(SLOTS):
                    own = local(flow[0], s, target_of(flow, k))
                    values.append([own[c] + decode(arrived, scale, 2, s, c) for c in range(2)])
                encode(values, send.at[f, k - 1])
                ring_copy(f, k).start()

        spread_codes(k)
        lax.fori_loop(4 * k - 3, jnp.minimum(4 * k + 1, N_EX), share_state, 0)

        @pl.when(k > LAG)
        def _():
            last_step(k - LAG)

        return carry

    lax.fori_loop(2, HOPS + 1, hop, 0)

    for part in range(LAST):
        last_step(HOPS - LAG + 1 + part)
        ends = []
        for f in (2 * part, 2 * part + 1):
            hops = FLOWS[f][2]
            ring_copy(f, hops).wait_recv()
            ends.append(recv.at[f, hops - 1])
        end_scales = [scale_of(end[pl.ds(4 * BLOCK, 16), :]) for end in ends]
        for s in range(SLOTS):
            own = local(part, s, z)
            for c in range(2):
                value = own[c]
                for end, scale in zip(ends, end_scales):
                    value = value + decode(end, scale, 2, s, c)
                sums[part, :, c, s] = value

        def share_sums(d, carry, part=part):
            j = lax.rem(me + d, N_EX)
            pltpu.make_async_remote_copy(
                src_ref=sums.at[part, j // 2, lax.rem(j, 2)],
                dst_ref=slots_in.at[part, me],
                send_sem=sums_send,
                recv_sem=sums_recv.at[part],
                device_id=(z, j),
                device_id_type=MESH,
            ).start()
            return carry

        lax.fori_loop(1, N_EX, share_sums, 0)
        pltpu.make_async_copy(
            sums.at[part, my_group, my_half], slots_in.at[part, me], sums_recv.at[part]
        ).start()

    my_rows = pl.ds(pl.multiple_of(8 * my_group, 8), 8)

    def apply(part, total):
        columns = slice(LANES * part, LANES * (part + 1))
        grad = total * (1.0 / math.sqrt(N_DP * CAP))
        weight = state[0, :, :, columns].reshape(8 * N_EX, LANES)
        first = 0.8 * state[1, :, :, columns].reshape(8 * N_EX, LANES) + 0.2 * grad
        second = 0.95 * state[2, :, :, columns].reshape(8 * N_EX, LANES) + 0.05 * grad * grad
        new = weight - 0.3 * (first / (jnp.sqrt(second) + 1e-08) + 0.1 * weight)
        fresh[part] = new.reshape(N_EX, 8, LANES)
        spread = lax.dot_general(
            pick[...],
            new.astype(jnp.bfloat16),
            (((0,), (0,)), ((), ())),
            preferred_element_type=jnp.float32,
        )
        hosted[part] = spread.astype(jnp.bfloat16).reshape(N_EX, 16, LANES)
        at = pl.ds(pl.multiple_of(HALF * my_half + LANES * part, LANES), LANES)

        def share_new(d, carry):
            j = lax.rem(me + d, N_EX)
            pltpu.make_async_remote_copy(
                src_ref=fresh.at[part, j],
                dst_ref=new_in.at[my_rows, at],
                send_sem=new_send,
                recv_sem=new_recv,
                device_id=(z, j),
                device_id_type=MESH,
            ).start()
            pltpu.make_async_remote_copy(
                src_ref=hosted.at[part, j],
                dst_ref=hosted_in.at[my_group, :, at],
                send_sem=hosted_send,
                recv_sem=hosted_recv,
                device_id=(z, j),
                device_id_type=MESH,
            ).start()
            return carry

        lax.fori_loop(1, N_EX, share_new, 0)
        pltpu.make_async_copy(fresh.at[part, me], new_in.at[my_rows, at], new_recv).start()
        pltpu.make_async_copy(
            hosted.at[part, me], hosted_in.at[my_group, :, at], hosted_recv
        ).start()

    pltpu.make_async_copy(state, state, state_recv).wait()
    for k in range(HOPS - LAG + LAST + 1, HOPS + 1):
        last_step(k)

    for part in range(LAST):
        pltpu.make_async_copy(slots_in.at[part], slots_in.at[part], sums_recv.at[part]).wait()
        value = slots_in[part].reshape(8 * SLOTS * N_EX, LANES)
        total = jnp.zeros((8 * N_EX, LANES), jnp.float32)
        for _ in range(3):
            piece = value.astype(jnp.bfloat16)
            value = value - piece.astype(jnp.float32)
            total = total + jnp.dot(pick[...], piece, preferred_element_type=jnp.float32)
        apply(part, total)

    last_copy(0, HOPS).wait_recv()
    up = last_arrived(0, HOPS)
    apply(
        LAST,
        jnp.concatenate([(last_own[g] + up[g]).reshape(BLOCK, LANES) for g in range(2)], axis=0),
    )

    pltpu.make_async_copy(new_in, new_in, new_recv).wait()
    pltpu.make_async_copy(hosted_in, hosted_in, hosted_recv).wait()

    for f, flow in enumerate(FLOWS):
        for k in range(1, flow[2] + 1):
            ring_copy(f, k).wait_send()
    for f, flow in enumerate(LAST_FLOWS):
        for k in range(1, flow[2] + 1):
            last_copy(f, k).wait_send()
    others = pl.ds(0, N_EX - 1)
    for sent, sem in (
        (level_in.at[others], level_send),
        (code_in.at[others], code_send),
        (state.at[:, others], state_send),
        (slots_in.at[:, others], sums_send),
        (fresh.at[:, others], new_send),
        (hosted.at[:, others], hosted_send),
    ):
        pltpu.make_async_copy(sent, sent, sem).wait()


def unpack(new_in, hosted_in, new_ref, weights_ref):
    new_ref[...] = new_in[...]
    for pair in range(8):
        both = [hosted_in[2 * pair + i].astype(jnp.float32) for i in range(2)]
        for s in range(SLOTS):
            block = jnp.concatenate([b[8 * s : 8 * s + 8] for b in both], axis=0)
            weights_ref[s, 16 * pair : 16 * pair + 16, :] = block.astype(jnp.bfloat16)


def body(x_rows, dy_rows, counts, host_table, owned, master, moment1, moment2):
    vmem = pl.BlockSpec(memory_space=pltpu.VMEM)
    hbm = pl.BlockSpec(memory_space=pltpu.HBM)
    dma = pltpu.SemaphoreType.DMA
    flows = len(FLOWS)
    new_pieces, hosted_pieces = pl.pallas_call(
        kernel,
        out_shape=(
            jax.ShapeDtypeStruct((BLOCK, FEATS), jnp.float32),
            jax.ShapeDtypeStruct((16, 16, FEATS), jnp.bfloat16),
        ),
        in_specs=[hbm] * 8,
        out_specs=(hbm, hbm),
        scratch_shapes=[
            pltpu.VMEM((SLOTS, CAP, WIDTH), jnp.bfloat16),
            pltpu.VMEM((SLOTS, CAP, FEATS), jnp.bfloat16),
            pltpu.SMEM((SLOTS,), jnp.int32),
            pltpu.SMEM((SLOTS, N_EX), jnp.int32),
            pltpu.SMEM((N_EX,), jnp.int32),
            pltpu.VMEM((3, BLOCK, FEATS), jnp.float32),
            pltpu.VMEM((PARTS, SLOTS, CAP, 2 * LANES), jnp.bfloat16),
            pltpu.VMEM((flows, HOPS, CHUNK, LANES), jnp.int16),
            pltpu.VMEM((flows, HOPS, CHUNK, LANES), jnp.int16),
            pltpu.VMEM((2, HOPS, LAST_CHUNK, LANES), jnp.int16),
            pltpu.VMEM((2, HOPS + 1, LAST_CHUNK, LANES), jnp.int16),
            pltpu.VMEM((2, 16, 8, LANES), jnp.float32),
            pltpu.VMEM((2 * HOPS, SLOTS, 2, 16, 8, LANES), jnp.float32),
            pltpu.VMEM((SLOTS, 2, 16, 8, LANES), jnp.float32),
            pltpu.VMEM((16, 2, 16, LANES), jnp.int16),
            pltpu.VMEM((N_EX, 16, LANES), jnp.int16),
            pltpu.VMEM((N_EX, 16, LANES), jnp.float32),
            pltpu.VMEM((16, 2, 2 * HOPS, 16, LANES), jnp.int16),
            pltpu.VMEM((N_EX, 2 * HOPS, 16, LANES), jnp.int16),
            pltpu.VMEM((8 * N_EX, 8 * SLOTS * N_EX), jnp.bfloat16),
            pltpu.VMEM((LAST, 16, 2, SLOTS, 8, LANES), jnp.float32),
            pltpu.VMEM((LAST, N_EX, SLOTS, 8, LANES), jnp.float32),
            pltpu.VMEM((3, N_EX, 8, HALF), jnp.float32),
            pltpu.VMEM((PARTS, N_EX, 8, LANES), jnp.float32),
            pltpu.VMEM((PARTS, N_EX, 16, LANES), jnp.bfloat16),
            dma((8,)),
            dma((flows, HOPS)),
            dma((flows, HOPS)),
            dma((2, HOPS)),
            dma((2, HOPS)),
            dma,
            dma,
            dma,
            dma((HOPS,)),
            dma,
            dma,
            dma,
            dma((LAST,)),
            dma,
            dma,
            dma,
            dma,
        ],
        compiler_params=pltpu.CompilerParams(
            collective_id=0, has_side_effects=True, vmem_limit_bytes=62 * 1024 * 1024
        ),
    )(
        x_rows[0], dy_rows[0], counts.reshape(SLOTS), host_table.T, owned,
        master[0], moment1[0], moment2[0],
    )
    new_master, host_weights = pl.pallas_call(
        unpack,
        out_shape=(
            jax.ShapeDtypeStruct((BLOCK, FEATS), jnp.float32),
            jax.ShapeDtypeStruct((SLOTS, BLOCK, FEATS), jnp.bfloat16),
        ),
        in_specs=[vmem, vmem],
        out_specs=(vmem, vmem),
        compiler_params=pltpu.CompilerParams(vmem_limit_bytes=62 * 1024 * 1024),
    )(new_pieces, hosted_pieces)
    return (new_master[None], host_weights[None])


def solution(mesh):
    in_specs = (
        P("expert", None, "dp", None),
        P("expert", None, "dp", None),
        P("expert", None, "dp"),
        P(),
        P(),
        P("expert", "dp", None),
        P("expert", "dp", None),
        P("expert", "dp", None),
    )
    out_specs = (P("expert", "dp", None), P("expert", None, "dp", None))
    return jax.shard_map(body, mesh=mesh, in_specs=in_specs, out_specs=out_specs, check_vma=False)
```

```python
import math

import jax
import jax.numpy as jnp
from jax import lax
from jax.experimental import pallas as pl
from jax.experimental.pallas import tpu as pltpu
from jax.sharding import PartitionSpec as P

N_DP = 16
N_EX = 32
SLOTS = 2
CAP = 256
WIDTH = 2048
BLOCK = 128
FEATS = 768
HALF = 384
PARTS = 3
LANES = 128
LAST = 2
HOPS = 8
LAG = 3
TOP = 32600.0
PER_OCTAVE = 256.0
KNEE = 2.0
FINE = 2000.0
MESH = pl.DeviceIdType.MESH
FLOWS = ((0, 1, 8), (0, -1, 7), (1, 1, 7), (1, -1, 8))
LAST_FLOWS = ((LAST, 1, 8), (LAST, -1, 7))
CHUNK = 4 * BLOCK + 16
LAST_CHUNK = 2 * BLOCK + 16


def level_of(peak):
    return jnp.ceil(jnp.log2(jnp.maximum(peak, 1e-20)) * PER_OCTAVE)


def to_code(value):
    return jnp.floor(value + 0.5).astype(jnp.int32).astype(jnp.int16)


def to_float(code):
    return code.astype(jnp.int32).astype(jnp.float32)


def encode(values, buf):
    count = len(values[0])
    peaks = []
    for group in values:
        peak = jnp.max(jnp.abs(group[0]), axis=0)
        for value in group[1:]:
            peak = jnp.maximum(peak, jnp.max(jnp.abs(value), axis=0))
        peaks.append(peak)
    level = level_of(jnp.concatenate(peaks, axis=0))
    inverse = jnp.exp2(level * (-1.0 / PER_OCTAVE)) * TOP
    buf[pl.ds(2 * count * BLOCK, 16), :] = level.astype(jnp.int32).astype(jnp.int16)
    for s, group in enumerate(values):
        for c, value in enumerate(group):
            code = to_code(value * inverse[8 * s : 8 * s + 8][None])
            buf[pl.ds((count * s + c) * BLOCK, BLOCK), :] = code.reshape(BLOCK, LANES)


def scale_of(level):
    return jnp.exp2(to_float(level) * (1.0 / PER_OCTAVE)) * (1.0 / TOP)


def decode(buf, scale, count, s, c):
    code = to_float(buf[pl.ds((count * s + c) * BLOCK, BLOCK), :])
    return code.reshape(16, 8, LANES) * scale[8 * s : 8 * s + 8][None]


def compress(value):
    code = jnp.floor(jnp.log2(1.0 + jnp.abs(value) * (1.0 / KNEE)) * FINE + 0.5)
    return jnp.where(value < 0.0, -code, code)


def expand(code):
    code = to_float(code)
    size = (jnp.exp2(jnp.abs(code) * (1.0 / FINE)) - 1.0) * KNEE
    return jnp.where(code < 0.0, -size, size)


def kernel(
    x_hbm, dy_hbm, counts_hbm, table_hbm, owned_hbm, master_hbm, first_hbm, second_hbm,
    new_in, hosted_in,
    x_ref, dy_ref, counts_ref, table_ref, owned_ref, mine,
    kept, send, recv, last_send, last_recv, last_own,
    early, early_inverse, level_out, level_in, early_scale, code_out, code_in,
    pick, sums, slots_in, state, fresh, hosted,
    load_sem, ring_send, ring_recv, last_ring_send, last_ring_recv,
    level_send, level_recv, code_send, code_recv, state_send, state_recv,
    sums_send, sums_recv, new_send, new_recv, hosted_send, hosted_recv,
):
    z = lax.axis_index("dp")
    me = lax.axis_index("expert")
    my_group = me // 2
    my_half = lax.rem(me, 2)

    loads = [
        pltpu.make_async_copy(src, dst, load_sem.at[i])
        for i, (src, dst) in enumerate(
            (
                (counts_hbm, counts_ref),
                (dy_hbm, dy_ref),
                (x_hbm, x_ref),
                (table_hbm, table_ref),
                (owned_hbm, owned_ref),
                (master_hbm, mine.at[0]),
                (first_hbm, mine.at[1]),
                (second_hbm, mine.at[2]),
            )
        )
    ]
    for load in loads:
        load.start()

    barrier = pltpu.get_barrier_semaphore()
    for step in (1, N_DP - 1):
        pl.semaphore_signal(
            barrier, inc=1, device_id=(lax.rem(z + step, N_DP), me), device_id_type=MESH
        )

    def greet(d, carry):
        pl.semaphore_signal(
            barrier, inc=1, device_id=(z, lax.rem(me + d, N_EX)), device_id_type=MESH
        )
        return carry

    lax.fori_loop(1, N_EX, greet, 0)

    def keep(part):
        rows = lax.broadcasted_iota(jnp.int32, (CAP, LANES), 0)
        for s in range(SLOTS):
            live = (rows < counts_ref[s]).astype(jnp.float32)
            for c in range(2):
                at = HALF * c + LANES * part
                value = dy_ref[s, :, at : at + LANES].astype(jnp.float32) * live
                kept[part, s, :, c * LANES : (c + 1) * LANES] = value.astype(jnp.bfloat16)

    def local(part, s, target):
        columns = pl.ds(pl.multiple_of(target * BLOCK, BLOCK), BLOCK)
        product = lax.dot_general(
            x_ref[s, :, columns],
            kept[part, s],
            (((0,), (0,)), ((), ())),
            preferred_element_type=jnp.float32,
        )
        return [product[:, c * LANES : (c + 1) * LANES].reshape(16, 8, LANES) for c in range(2)]

    def neighbour(sign):
        return (lax.rem(z + sign + N_DP, N_DP), me)

    def target_of(flow, k):
        _, sign, hops = flow
        return lax.rem(z + sign * (hops + 1 - k) + N_DP, N_DP)

    def ring_copy(f, k):
        return pltpu.make_async_remote_copy(
            src_ref=send.at[f, k - 1],
            dst_ref=recv.at[f, k - 1],
            send_sem=ring_send.at[f, k - 1],
            recv_sem=ring_recv.at[f, k - 1],
            device_id=neighbour(FLOWS[f][1]),
            device_id_type=MESH,
        )

    def last_copy(f, k):
        return pltpu.make_async_remote_copy(
            src_ref=last_send.at[f, k - 1],
            dst_ref=last_recv.at[f, k],
            send_sem=last_ring_send.at[f, k - 1],
            recv_sem=last_ring_recv.at[f, k - 1],
            device_id=neighbour(LAST_FLOWS[f][1]),
            device_id_type=MESH,
        )

    for load in loads[:3]:
        load.wait()
    for f, flow in enumerate(FLOWS):
        if f % 2 == 0:
            keep(flow[0])
        encode([local(flow[0], s, target_of(flow, 1)) for s in range(SLOTS)], send.at[f, 0])
        if f == 0:
            pl.semaphore_wait(barrier, N_EX - 1 + 2)
        ring_copy(f, 1).start()
    keep(LAST)

    for s in range(SLOTS):
        for c in range(2):
            early_inverse[s, c] = jnp.zeros((16, 8, LANES), jnp.float32)

    def multiply(k, carry):
        for i, flow in enumerate(LAST_FLOWS):
            for s in range(SLOTS):
                products = local(LAST, s, target_of(flow, k))
                for c in range(2):
                    early[2 * (k - 1) + i, s, c] = products[c]
                    early_inverse[s, c] = jnp.maximum(early_inverse[s, c], jnp.abs(products[c]))
        return carry

    lax.fori_loop(1, HOPS + 1, multiply, 0)
    for c in range(2):
        levels = []
        for s in range(SLOTS):
            level = level_of(early_inverse[s, c])
            early_inverse[s, c] = jnp.exp2(level * (-1.0 / PER_OCTAVE)) * TOP
            levels.append(level)
        level_out[:, c] = jnp.concatenate(levels, axis=1).astype(jnp.int32).astype(jnp.int16)

    def share_levels(d, carry):
        j = lax.rem(me + d, N_EX)
        pltpu.make_async_remote_copy(
            src_ref=level_out.at[j // 2, lax.rem(j, 2)],
            dst_ref=level_in.at[me],
            send_sem=level_send,
            recv_sem=level_recv,
            device_id=(z, j),
            device_id_type=MESH,
        ).start()
        return carry

    lax.fori_loop(1, N_EX, share_levels, 0)
    pltpu.make_async_copy(level_out.at[my_group, my_half], level_in.at[me], level_recv).start()

    def spread_codes(k):
        both = pl.ds(2 * (k - 1), 2)
        for i in range(2):
            o = 2 * (k - 1) + i
            for c in range(2):
                codes = [
                    jnp.floor(early[o, s, c] * early_inverse[s, c] + 0.5) for s in range(SLOTS)
                ]
                code = jnp.concatenate(codes, axis=1).astype(jnp.int32).astype(jnp.int16)
                code_out[:, c, o] = code

        def share_codes(d, carry):
            j = lax.rem(me + d, N_EX)
            pltpu.make_async_remote_copy(
                src_ref=code_out.at[j // 2, lax.rem(j, 2), both],
                dst_ref=code_in.at[me, both],
                send_sem=code_send,
                recv_sem=code_recv.at[k - 1],
                device_id=(z, j),
                device_id_type=MESH,
            ).start()
            return carry

        lax.fori_loop(1, N_EX, share_codes, 0)
        pltpu.make_async_copy(
            code_out.at[my_group, my_half, both], code_in.at[me, both], code_recv.at[k - 1]
        ).start()

    def share_state(d, carry):
        j = lax.rem(me + d, N_EX)
        rows_of = pl.ds(pl.multiple_of(8 * (j // 2), 8), 8)
        columns_of = pl.ds(pl.multiple_of(HALF * lax.rem(j, 2), LANES), HALF)
        for a in range(3):
            pltpu.make_async_remote_copy(
                src_ref=mine.at[a, rows_of, columns_of],
                dst_ref=state.at[a, me],
                send_sem=state_send,
                recv_sem=state_recv,
                device_id=(z, j),
                device_id_type=MESH,
            ).start()
        return carry

    def merge_early(k):
        both = pl.ds(2 * (k - 1), 2)
        arrived = code_in.at[:, both]
        pltpu.make_async_copy(arrived, arrived, code_recv.at[k - 1]).wait()
        high = []
        low = []
        for i in range(2):
            value = to_float(code_in[:, 2 * (k - 1) + i]) * early_scale[...]
            value = value.reshape(8 * SLOTS * N_EX, LANES)
            top = value.astype(jnp.bfloat16)
            high.append(top)
            low.append((value - top.astype(jnp.float32)).astype(jnp.bfloat16))
        merged = jnp.dot(
            pick[...], jnp.concatenate(high, axis=1), preferred_element_type=jnp.float32
        ) + jnp.dot(pick[...], jnp.concatenate(low, axis=1), preferred_element_type=jnp.float32)
        return [merged[:, i * LANES : (i + 1) * LANES].reshape(2, 16, 8, LANES) for i in range(2)]

    def last_arrived(f, k):
        buf = last_recv.at[f, k]
        scale = scale_of(buf[pl.ds(2 * BLOCK, 16), :])
        return [decode(buf, scale, 1, g, 0) for g in range(2)]

    def last_step(k):
        merged = merge_early(k)

        @pl.when(k > 1)
        def _():
            last_copy(0, k - 1).wait_recv()

        arrived = last_arrived(0, k - 1)
        encode([[merged[0][g] + arrived[g]] for g in range(2)], last_send.at[0, k - 1])
        last_copy(0, k).start()

        @pl.when(k > 1)
        def _():
            last_copy(1, k - 1).wait_recv()

        arrived = last_arrived(1, k - 1)
        values = [merged[1][g] + arrived[g] for g in range(2)]

        @pl.when(k < HOPS)
        def _():
            encode([[value] for value in values], last_send.at[1, k - 1])
            last_copy(1, k).start()

        @pl.when(k == HOPS)
        def _():
            for g in range(2):
                last_own[g] = values[g]

    last_recv[:, 0] = jnp.zeros((2, LAST_CHUNK, LANES), jnp.int16)
    spread_codes(1)
    spread_codes(2)

    for load in loads[3:]:
        load.wait()
    lane = lax.broadcasted_iota(jnp.int32, (16, 8 * SLOTS * N_EX), 1)
    row = lax.broadcasted_iota(jnp.int32, (16, 8 * SLOTS * N_EX), 0)

    def fill(h, names):
        for s in range(SLOTS):
            names = jnp.where(lane // 8 == h * SLOTS + s, table_ref[s, h], names)
        return names

    names = lax.fori_loop(0, N_EX, fill, jnp.zeros_like(lane))

    def fill_pick(pair, carry):
        expert = jnp.where(row < 8, owned_ref[2 * pair], owned_ref[2 * pair + 1])
        same = jnp.where((names == expert) & (lane % 8 == row % 8), 1.0, 0.0)
        pick[pl.ds(pl.multiple_of(16 * pair, 16), 16), :] = same.astype(jnp.bfloat16)
        return carry

    lax.fori_loop(0, N_EX // 2, fill_pick, 0)

    lax.fori_loop(1, 5, share_state, 0)
    for a in range(3):
        pltpu.make_async_copy(
            mine.at[
                a,
                pl.ds(pl.multiple_of(8 * my_group, 8), 8),
                pl.ds(pl.multiple_of(HALF * my_half, LANES), HALF),
            ],
            state.at[a, me],
            state_recv,
        ).start()
    pltpu.make_async_copy(level_in, level_in, level_recv).wait()
    early_scale[...] = scale_of(level_in[...])
    def hop(k, carry):
        @pl.when(k > LAG)
        def _():
            last_step(k - LAG)

        for f, flow in enumerate(FLOWS):

            @pl.when(k <= flow[2])
            def _(f=f, flow=flow):
                ring_copy(f, k - 1).wait_recv()
                arrived = recv.at[f, k - 2]
                scale = scale_of(arrived[pl.ds(4 * BLOCK, 16), :])
                values = []
                for s in range(SLOTS):
                    own = local(flow[0], s, target_of(flow, k))
                    values.append([own[c] + decode(arrived, scale, 2, s, c) for c in range(2)])
                encode(values, send.at[f, k - 1])
                ring_copy(f, k).start()

        @pl.when(k < HOPS)
        def _():
            spread_codes(k + 1)

        lax.fori_loop(4 * k - 3, jnp.minimum(4 * k + 1, N_EX), share_state, 0)

        return carry

    lax.fori_loop(2, HOPS + 1, hop, 0)

    for part in range(LAST):
        last_step(HOPS - LAG + 1 + part)
        ends = []
        for f in (2 * part, 2 * part + 1):
            hops = FLOWS[f][2]
            ring_copy(f, hops).wait_recv()
            ends.append(recv.at[f, hops - 1])
        end_scales = [scale_of(end[pl.ds(4 * BLOCK, 16), :]) for end in ends]
        codes = [[], []]
        for s in range(SLOTS):
            own = local(part, s, z)
            for c in range(2):
                value = own[c]
                for end, scale in zip(ends, end_scales):
                    value = value + decode(end, scale, 2, s, c)
                codes[c].append(compress(value))
        for c in range(2):
            code = jnp.concatenate(codes[c], axis=1)
            sums[part, :, c] = code.astype(jnp.int32).astype(jnp.int16)

        def share_sums(d, carry, part=part):
            j = lax.rem(me + d, N_EX)
            pltpu.make_async_remote_copy(
                src_ref=sums.at[part, j // 2, lax.rem(j, 2)],
                dst_ref=slots_in.at[part, me],
                send_sem=sums_send,
                recv_sem=sums_recv.at[part],
                device_id=(z, j),
                device_id_type=MESH,
            ).start()
            return carry

        lax.fori_loop(1, N_EX, share_sums, 0)
        pltpu.make_async_copy(
            sums.at[part, my_group, my_half], slots_in.at[part, me], sums_recv.at[part]
        ).start()

    my_rows = pl.ds(pl.multiple_of(8 * my_group, 8), 8)

    def apply(part, total):
        columns = slice(LANES * part, LANES * (part + 1))
        grad = total * (1.0 / math.sqrt(N_DP * CAP))
        weight = state[0, :, :, columns].reshape(8 * N_EX, LANES)
        first = 0.8 * state[1, :, :, columns].reshape(8 * N_EX, LANES) + 0.2 * grad
        second = 0.95 * state[2, :, :, columns].reshape(8 * N_EX, LANES) + 0.05 * grad * grad
        new = weight - 0.3 * (first / (jnp.sqrt(second) + 1e-08) + 0.1 * weight)
        fresh[part] = new.reshape(N_EX, 8, LANES)
        spread = lax.dot_general(
            pick[...],
            new.astype(jnp.bfloat16),
            (((0,), (0,)), ((), ())),
            preferred_element_type=jnp.float32,
        )
        hosted[part] = spread.astype(jnp.bfloat16).reshape(N_EX, 16, LANES)
        at = pl.ds(pl.multiple_of(HALF * my_half + LANES * part, LANES), LANES)

        def share_new(d, carry):
            j = lax.rem(me + d, N_EX)
            pltpu.make_async_remote_copy(
                src_ref=fresh.at[part, j],
                dst_ref=new_in.at[my_rows, at],
                send_sem=new_send,
                recv_sem=new_recv,
                device_id=(z, j),
                device_id_type=MESH,
            ).start()
            pltpu.make_async_remote_copy(
                src_ref=hosted.at[part, j],
                dst_ref=hosted_in.at[my_group, :, at],
                send_sem=hosted_send,
                recv_sem=hosted_recv,
                device_id=(z, j),
                device_id_type=MESH,
            ).start()
            return carry

        lax.fori_loop(1, N_EX, share_new, 0)
        pltpu.make_async_copy(fresh.at[part, me], new_in.at[my_rows, at], new_recv).start()
        pltpu.make_async_copy(
            hosted.at[part, me], hosted_in.at[my_group, :, at], hosted_recv
        ).start()

    pltpu.make_async_copy(state, state, state_recv).wait()
    for k in range(HOPS - LAG + LAST + 1, HOPS + 1):
        last_step(k)

    for part in range(LAST):
        pltpu.make_async_copy(slots_in.at[part], slots_in.at[part], sums_recv.at[part]).wait()
        value = expand(slots_in[part]).reshape(8 * SLOTS * N_EX, LANES)
        total = jnp.zeros((8 * N_EX, LANES), jnp.float32)
        for _ in range(3):
            piece = value.astype(jnp.bfloat16)
            value = value - piece.astype(jnp.float32)
            total = total + jnp.dot(pick[...], piece, preferred_element_type=jnp.float32)
        apply(part, total)

    last_copy(0, HOPS).wait_recv()
    up = last_arrived(0, HOPS)
    apply(
        LAST,
        jnp.concatenate([(last_own[g] + up[g]).reshape(BLOCK, LANES) for g in range(2)], axis=0),
    )

    pltpu.make_async_copy(new_in, new_in, new_recv).wait()
    pltpu.make_async_copy(hosted_in, hosted_in, hosted_recv).wait()

    for f, flow in enumerate(FLOWS):
        for k in range(1, flow[2] + 1):
            ring_copy(f, k).wait_send()
    for f, flow in enumerate(LAST_FLOWS):
        for k in range(1, flow[2] + 1):
            last_copy(f, k).wait_send()
    others = pl.ds(0, N_EX - 1)
    for sent, sem in (
        (level_in.at[others], level_send),
        (code_in.at[others], code_send),
        (state.at[:, others], state_send),
        (slots_in.at[:, others], sums_send),
        (fresh.at[:, others], new_send),
        (hosted.at[:, others], hosted_send),
    ):
        pltpu.make_async_copy(sent, sent, sem).wait()


def unpack(new_in, hosted_in, new_ref, weights_ref):
    new_ref[...] = new_in[...]
    for pair in range(8):
        both = [hosted_in[2 * pair + i].astype(jnp.float32) for i in range(2)]
        for s in range(SLOTS):
            block = jnp.concatenate([b[8 * s : 8 * s + 8] for b in both], axis=0)
            weights_ref[s, 16 * pair : 16 * pair + 16, :] = block.astype(jnp.bfloat16)


def body(x_rows, dy_rows, counts, host_table, owned, master, moment1, moment2):
    vmem = pl.BlockSpec(memory_space=pltpu.VMEM)
    hbm = pl.BlockSpec(memory_space=pltpu.HBM)
    dma = pltpu.SemaphoreType.DMA
    flows = len(FLOWS)
    new_pieces, hosted_pieces = pl.pallas_call(
        kernel,
        out_shape=(
            jax.ShapeDtypeStruct((BLOCK, FEATS), jnp.float32),
            jax.ShapeDtypeStruct((16, 16, FEATS), jnp.bfloat16),
        ),
        in_specs=[hbm] * 8,
        out_specs=(hbm, hbm),
        scratch_shapes=[
            pltpu.VMEM((SLOTS, CAP, WIDTH), jnp.bfloat16),
            pltpu.VMEM((SLOTS, CAP, FEATS), jnp.bfloat16),
            pltpu.SMEM((SLOTS,), jnp.int32),
            pltpu.SMEM((SLOTS, N_EX), jnp.int32),
            pltpu.SMEM((N_EX,), jnp.int32),
            pltpu.VMEM((3, BLOCK, FEATS), jnp.float32),
            pltpu.VMEM((PARTS, SLOTS, CAP, 2 * LANES), jnp.bfloat16),
            pltpu.VMEM((flows, HOPS, CHUNK, LANES), jnp.int16),
            pltpu.VMEM((flows, HOPS, CHUNK, LANES), jnp.int16),
            pltpu.VMEM((2, HOPS, LAST_CHUNK, LANES), jnp.int16),
            pltpu.VMEM((2, HOPS + 1, LAST_CHUNK, LANES), jnp.int16),
            pltpu.VMEM((2, 16, 8, LANES), jnp.float32),
            pltpu.VMEM((2 * HOPS, SLOTS, 2, 16, 8, LANES), jnp.float32),
            pltpu.VMEM((SLOTS, 2, 16, 8, LANES), jnp.float32),
            pltpu.VMEM((16, 2, 16, LANES), jnp.int16),
            pltpu.VMEM((N_EX, 16, LANES), jnp.int16),
            pltpu.VMEM((N_EX, 16, LANES), jnp.float32),
            pltpu.VMEM((16, 2, 2 * HOPS, 16, LANES), jnp.int16),
            pltpu.VMEM((N_EX, 2 * HOPS, 16, LANES), jnp.int16),
            pltpu.VMEM((8 * N_EX, 8 * SLOTS * N_EX), jnp.bfloat16),
            pltpu.VMEM((LAST, 16, 2, 16, LANES), jnp.int16),
            pltpu.VMEM((LAST, N_EX, 16, LANES), jnp.int16),
            pltpu.VMEM((3, N_EX, 8, HALF), jnp.float32),
            pltpu.VMEM((PARTS, N_EX, 8, LANES), jnp.float32),
            pltpu.VMEM((PARTS, N_EX, 16, LANES), jnp.bfloat16),
            dma((8,)),
            dma((flows, HOPS)),
            dma((flows, HOPS)),
            dma((2, HOPS)),
            dma((2, HOPS)),
            dma,
            dma,
            dma,
            dma((HOPS,)),
            dma,
            dma,
            dma,
            dma((LAST,)),
            dma,
            dma,
            dma,
            dma,
        ],
        compiler_params=pltpu.CompilerParams(
            collective_id=0, has_side_effects=True, vmem_limit_bytes=62 * 1024 * 1024
        ),
    )(
        x_rows[0], dy_rows[0], counts.reshape(SLOTS), host_table.T, owned,
        master[0], moment1[0], moment2[0],
    )
    new_master, host_weights = pl.pallas_call(
        unpack,
        out_shape=(
            jax.ShapeDtypeStruct((BLOCK, FEATS), jnp.float32),
            jax.ShapeDtypeStruct((SLOTS, BLOCK, FEATS), jnp.bfloat16),
        ),
        in_specs=[vmem, vmem],
        out_specs=(vmem, vmem),
        compiler_params=pltpu.CompilerParams(vmem_limit_bytes=62 * 1024 * 1024),
    )(new_pieces, hosted_pieces)
    return (new_master[None], host_weights[None])


def solution(mesh):
    in_specs = (
        P("expert", None, "dp", None),
        P("expert", None, "dp", None),
        P("expert", None, "dp"),
        P(),
        P(),
        P("expert", "dp", None),
        P("expert", "dp", None),
        P("expert", "dp", None),
    )
    out_specs = (P("expert", "dp", None), P("expert", None, "dp", None))
    return jax.shard_map(body, mesh=mesh, in_specs=in_specs, out_specs=out_specs, check_vma=False)
```

```python
import math

import jax
import jax.numpy as jnp
from jax import lax
from jax.experimental import pallas as pl
from jax.experimental.pallas import tpu as pltpu
from jax.sharding import PartitionSpec as P

N_DP = 16
N_EX = 32
SLOTS = 2
CAP = 256
WIDTH = 2048
BLOCK = 128
FEATS = 768
HALF = 384
PARTS = 3
LANES = 128
LAST = 2
HOPS = 8
LAG = 3
TOP = 32600.0
PER_OCTAVE = 256.0
KNEE = 2.0
FINE = 2000.0
MESH = pl.DeviceIdType.MESH
FLOWS = ((0, 1, 8), (0, -1, 7), (1, 1, 7), (1, -1, 8))
LAST_FLOWS = ((LAST, 1, 8), (LAST, -1, 7))
CHUNK = 4 * BLOCK + 16
LAST_CHUNK = 2 * BLOCK + 16


def level_of(peak):
    return jnp.ceil(jnp.log2(jnp.maximum(peak, 1e-20)) * PER_OCTAVE)


def to_code(value):
    return jnp.floor(value + 0.5).astype(jnp.int32).astype(jnp.int16)


def to_float(code):
    return code.astype(jnp.int32).astype(jnp.float32)


def encode(values, buf):
    count = len(values[0])
    peaks = []
    for group in values:
        peak = jnp.max(jnp.abs(group[0]), axis=0)
        for value in group[1:]:
            peak = jnp.maximum(peak, jnp.max(jnp.abs(value), axis=0))
        peaks.append(peak)
    level = level_of(jnp.concatenate(peaks, axis=0))
    inverse = jnp.exp2(level * (-1.0 / PER_OCTAVE)) * TOP
    buf[pl.ds(2 * count * BLOCK, 16), :] = level.astype(jnp.int32).astype(jnp.int16)
    for s, group in enumerate(values):
        for c, value in enumerate(group):
            code = to_code(value * inverse[8 * s : 8 * s + 8][None])
            buf[pl.ds((count * s + c) * BLOCK, BLOCK), :] = code.reshape(BLOCK, LANES)


def scale_of(level):
    return jnp.exp2(to_float(level) * (1.0 / PER_OCTAVE)) * (1.0 / TOP)


def decode(buf, scale, count, s, c):
    code = to_float(buf[pl.ds((count * s + c) * BLOCK, BLOCK), :])
    return code.reshape(16, 8, LANES) * scale[8 * s : 8 * s + 8][None]


def compress(value):
    code = jnp.floor(jnp.log2(1.0 + jnp.abs(value) * (1.0 / KNEE)) * FINE + 0.5)
    return jnp.where(value < 0.0, -code, code)


def expand(code):
    code = to_float(code)
    size = (jnp.exp2(jnp.abs(code) * (1.0 / FINE)) - 1.0) * KNEE
    return jnp.where(code < 0.0, -size, size)


def kernel(
    x_hbm, dy_hbm, counts_hbm, table_hbm, owned_hbm, master_hbm, first_hbm, second_hbm,
    new_in, hosted_in,
    x_ref, dy_ref, counts_ref, table_ref, owned_ref, mine,
    kept, send, recv, last_send, last_recv, last_own,
    early, early_inverse, level_out, level_in, early_scale, code_out, code_in,
    pick, sums, slots_in, state, fresh, hosted,
    load_sem, ring_send, ring_recv, last_ring_send, last_ring_recv,
    level_send, level_recv, code_send, code_recv, state_send, state_recv,
    sums_send, sums_recv, new_send, new_recv, hosted_send, hosted_recv,
):
    z = lax.axis_index("dp")
    me = lax.axis_index("expert")
    my_group = me // 2
    my_half = lax.rem(me, 2)

    loads = [
        pltpu.make_async_copy(src, dst, load_sem.at[i])
        for i, (src, dst) in enumerate(
            (
                (counts_hbm, counts_ref),
                (dy_hbm, dy_ref),
                (x_hbm, x_ref),
                (table_hbm, table_ref),
                (owned_hbm, owned_ref),
                (master_hbm, mine.at[0]),
                (first_hbm, mine.at[1]),
                (second_hbm, mine.at[2]),
            )
        )
    ]
    for load in loads:
        load.start()

    barrier = pltpu.get_barrier_semaphore()
    for step in (1, N_DP - 1):
        pl.semaphore_signal(
            barrier, inc=1, device_id=(lax.rem(z + step, N_DP), me), device_id_type=MESH
        )

    def greet(d, carry):
        pl.semaphore_signal(
            barrier, inc=1, device_id=(z, lax.rem(me + d, N_EX)), device_id_type=MESH
        )
        return carry

    lax.fori_loop(1, N_EX, greet, 0)

    def keep(part):
        rows = lax.broadcasted_iota(jnp.int32, (CAP, LANES), 0)
        for s in range(SLOTS):
            live = (rows < counts_ref[s]).astype(jnp.float32)
            for c in range(2):
                at = HALF * c + LANES * part
                value = dy_ref[s, :, at : at + LANES].astype(jnp.float32) * live
                kept[part, s, :, c * LANES : (c + 1) * LANES] = value.astype(jnp.bfloat16)

    def local(part, s, target):
        columns = pl.ds(pl.multiple_of(target * BLOCK, BLOCK), BLOCK)
        product = lax.dot_general(
            x_ref[s, :, columns],
            kept[part, s],
            (((0,), (0,)), ((), ())),
            preferred_element_type=jnp.float32,
        )
        return [product[:, c * LANES : (c + 1) * LANES].reshape(16, 8, LANES) for c in range(2)]

    def neighbour(sign):
        return (lax.rem(z + sign + N_DP, N_DP), me)

    def target_of(flow, k):
        _, sign, hops = flow
        return lax.rem(z + sign * (hops + 1 - k) + N_DP, N_DP)

    def ring_copy(f, k):
        return pltpu.make_async_remote_copy(
            src_ref=send.at[f, k - 1],
            dst_ref=recv.at[f, k - 1],
            send_sem=ring_send.at[f, k - 1],
            recv_sem=ring_recv.at[f, k - 1],
            device_id=neighbour(FLOWS[f][1]),
            device_id_type=MESH,
        )

    def last_copy(f, k):
        return pltpu.make_async_remote_copy(
            src_ref=last_send.at[f, k - 1],
            dst_ref=last_recv.at[f, k],
            send_sem=last_ring_send.at[f, k - 1],
            recv_sem=last_ring_recv.at[f, k - 1],
            device_id=neighbour(LAST_FLOWS[f][1]),
            device_id_type=MESH,
        )

    for load in loads[:2]:
        load.wait()
    for f, flow in enumerate(FLOWS):
        if f % 2 == 0:
            keep(flow[0])
        if f == 0:
            loads[2].wait()
        encode([local(flow[0], s, target_of(flow, 1)) for s in range(SLOTS)], send.at[f, 0])
        if f == 0:
            pl.semaphore_wait(barrier, N_EX - 1 + 2)
        ring_copy(f, 1).start()
    keep(LAST)

    for s in range(SLOTS):
        for c in range(2):
            early_inverse[s, c] = jnp.zeros((16, 8, LANES), jnp.float32)

    def multiply(k, carry):
        for i, flow in enumerate(LAST_FLOWS):
            for s in range(SLOTS):
                products = local(LAST, s, target_of(flow, k))
                for c in range(2):
                    early[2 * (k - 1) + i, s, c] = products[c]
                    early_inverse[s, c] = jnp.maximum(early_inverse[s, c], jnp.abs(products[c]))
        return carry

    lax.fori_loop(1, HOPS + 1, multiply, 0)
    for c in range(2):
        levels = []
        for s in range(SLOTS):
            level = level_of(early_inverse[s, c])
            early_inverse[s, c] = jnp.exp2(level * (-1.0 / PER_OCTAVE)) * TOP
            levels.append(level)
        level_out[:, c] = jnp.concatenate(levels, axis=1).astype(jnp.int32).astype(jnp.int16)

    def share_levels(d, carry):
        j = lax.rem(me + d, N_EX)
        pltpu.make_async_remote_copy(
            src_ref=level_out.at[j // 2, lax.rem(j, 2)],
            dst_ref=level_in.at[me],
            send_sem=level_send,
            recv_sem=level_recv,
            device_id=(z, j),
            device_id_type=MESH,
        ).start()
        return carry

    lax.fori_loop(1, N_EX, share_levels, 0)
    pltpu.make_async_copy(level_out.at[my_group, my_half], level_in.at[me], level_recv).start()

    def spread_codes(k):
        both = pl.ds(2 * (k - 1), 2)
        for i in range(2):
            o = 2 * (k - 1) + i
            for c in range(2):
                codes = [
                    jnp.floor(early[o, s, c] * early_inverse[s, c] + 0.5) for s in range(SLOTS)
                ]
                code = jnp.concatenate(codes, axis=1).astype(jnp.int32).astype(jnp.int16)
                code_out[:, c, o] = code

        def share_codes(d, carry):
            j = lax.rem(me + d, N_EX)
            pltpu.make_async_remote_copy(
                src_ref=code_out.at[j // 2, lax.rem(j, 2), both],
                dst_ref=code_in.at[me, both],
                send_sem=code_send,
                recv_sem=code_recv.at[k - 1],
                device_id=(z, j),
                device_id_type=MESH,
            ).start()
            return carry

        lax.fori_loop(1, N_EX, share_codes, 0)
        pltpu.make_async_copy(
            code_out.at[my_group, my_half, both], code_in.at[me, both], code_recv.at[k - 1]
        ).start()

    def share_state(d, carry):
        j = lax.rem(me + d, N_EX)
        rows_of = pl.ds(pl.multiple_of(8 * (j // 2), 8), 8)
        columns_of = pl.ds(pl.multiple_of(HALF * lax.rem(j, 2), LANES), HALF)
        for a in range(3):
            pltpu.make_async_remote_copy(
                src_ref=mine.at[a, rows_of, columns_of],
                dst_ref=state.at[a, me],
                send_sem=state_send,
                recv_sem=state_recv,
                device_id=(z, j),
                device_id_type=MESH,
            ).start()
        return carry

    def merge_early(k):
        both = pl.ds(2 * (k - 1), 2)
        arrived = code_in.at[:, both]
        pltpu.make_async_copy(arrived, arrived, code_recv.at[k - 1]).wait()
        high = []
        low = []
        for i in range(2):
            value = to_float(code_in[:, 2 * (k - 1) + i]) * early_scale[...]
            value = value.reshape(8 * SLOTS * N_EX, LANES)
            top = value.astype(jnp.bfloat16)
            high.append(top)
            low.append((value - top.astype(jnp.float32)).astype(jnp.bfloat16))
        merged = jnp.dot(
            pick[...], jnp.concatenate(high, axis=1), preferred_element_type=jnp.float32
        ) + jnp.dot(pick[...], jnp.concatenate(low, axis=1), preferred_element_type=jnp.float32)
        return [merged[:, i * LANES : (i + 1) * LANES].reshape(2, 16, 8, LANES) for i in range(2)]

    def last_arrived(f, k):
        buf = last_recv.at[f, k]
        scale = scale_of(buf[pl.ds(2 * BLOCK, 16), :])
        return [decode(buf, scale, 1, g, 0) for g in range(2)]

    def last_step(k):
        merged = merge_early(k)

        @pl.when(k > 1)
        def _():
            last_copy(0, k - 1).wait_recv()

        arrived = last_arrived(0, k - 1)
        encode([[merged[0][g] + arrived[g]] for g in range(2)], last_send.at[0, k - 1])
        last_copy(0, k).start()

        @pl.when(k > 1)
        def _():
            last_copy(1, k - 1).wait_recv()

        arrived = last_arrived(1, k - 1)
        values = [merged[1][g] + arrived[g] for g in range(2)]

        @pl.when(k < HOPS)
        def _():
            encode([[value] for value in values], last_send.at[1, k - 1])
            last_copy(1, k).start()

        @pl.when(k == HOPS)
        def _():
            for g in range(2):
                last_own[g] = values[g]

    last_recv[:, 0] = jnp.zeros((2, LAST_CHUNK, LANES), jnp.int16)
    spread_codes(1)
    spread_codes(2)


    for load in loads[5:]:
        load.wait()
    lax.fori_loop(1, 5, share_state, 0)
    for a in range(3):
        pltpu.make_async_copy(
            mine.at[
                a,
                pl.ds(pl.multiple_of(8 * my_group, 8), 8),
                pl.ds(pl.multiple_of(HALF * my_half, LANES), HALF),
            ],
            state.at[a, me],
            state_recv,
        ).start()
    def prepare():
        for load in loads[3:5]:
            load.wait()
        lane = lax.broadcasted_iota(jnp.int32, (16, 8 * SLOTS * N_EX), 1)
        row = lax.broadcasted_iota(jnp.int32, (16, 8 * SLOTS * N_EX), 0)

        def fill(h, names):
            for s in range(SLOTS):
                names = jnp.where(lane // 8 == h * SLOTS + s, table_ref[s, h], names)
            return names

        names = lax.fori_loop(0, N_EX, fill, jnp.zeros_like(lane))

        def fill_pick(pair, carry):
            expert = jnp.where(row < 8, owned_ref[2 * pair], owned_ref[2 * pair + 1])
            same = jnp.where((names == expert) & (lane % 8 == row % 8), 1.0, 0.0)
            pick[pl.ds(pl.multiple_of(16 * pair, 16), 16), :] = same.astype(jnp.bfloat16)
            return carry

        lax.fori_loop(0, N_EX // 2, fill_pick, 0)
        pltpu.make_async_copy(level_in, level_in, level_recv).wait()
        early_scale[...] = scale_of(level_in[...])

    def hop(k, carry):
        @pl.when(k > LAG)
        def _():
            last_step(k - LAG)

        for f, flow in enumerate(FLOWS):

            @pl.when(k <= flow[2])
            def _(f=f, flow=flow):
                ring_copy(f, k - 1).wait_recv()
                arrived = recv.at[f, k - 2]
                scale = scale_of(arrived[pl.ds(4 * BLOCK, 16), :])
                values = []
                for s in range(SLOTS):
                    own = local(flow[0], s, target_of(flow, k))
                    values.append([own[c] + decode(arrived, scale, 2, s, c) for c in range(2)])
                encode(values, send.at[f, k - 1])
                ring_copy(f, k).start()

        @pl.when(k < HOPS)
        def _():
            spread_codes(k + 1)

        lax.fori_loop(4 * k - 3, jnp.minimum(4 * k + 1, N_EX), share_state, 0)

        @pl.when(k == 2)
        def _():
            prepare()

        return carry

    lax.fori_loop(2, HOPS + 1, hop, 0)

    last_step(HOPS - LAG + 1)
    for part in range(LAST):
        f = 2 * part if FLOWS[2 * part][2] < HOPS else 2 * part + 1
        ring_copy(f, HOPS - 1).wait_recv()
        end = recv.at[f, HOPS - 2]
        scale = scale_of(end[pl.ds(4 * BLOCK, 16), :])
        for s in range(SLOTS):
            own = local(part, s, z)
            for c in range(2):
                early[part, s, c] = own[c] + decode(end, scale, 2, s, c)

    for part in range(LAST):
        if part == 1 and LAG > 2:
            last_step(HOPS - LAG + 2)
        f = 2 * part if FLOWS[2 * part][2] == HOPS else 2 * part + 1
        ring_copy(f, HOPS).wait_recv()
        end = recv.at[f, HOPS - 1]
        scale = scale_of(end[pl.ds(4 * BLOCK, 16), :])
        codes = [
            [compress(early[part, s, c] + decode(end, scale, 2, s, c)) for s in range(SLOTS)]
            for c in range(2)
        ]
        for c in range(2):
            code = jnp.concatenate(codes[c], axis=1)
            sums[part, :, c] = code.astype(jnp.int32).astype(jnp.int16)

        def share_sums(d, carry, part=part):
            j = lax.rem(me + d, N_EX)
            pltpu.make_async_remote_copy(
                src_ref=sums.at[part, j // 2, lax.rem(j, 2)],
                dst_ref=slots_in.at[part, me],
                send_sem=sums_send,
                recv_sem=sums_recv.at[part],
                device_id=(z, j),
                device_id_type=MESH,
            ).start()
            return carry

        lax.fori_loop(1, N_EX, share_sums, 0)
        pltpu.make_async_copy(
            sums.at[part, my_group, my_half], slots_in.at[part, me], sums_recv.at[part]
        ).start()

    my_rows = pl.ds(pl.multiple_of(8 * my_group, 8), 8)

    def apply(part, total):
        columns = slice(LANES * part, LANES * (part + 1))
        grad = total * (1.0 / math.sqrt(N_DP * CAP))
        weight = state[0, :, :, columns].reshape(8 * N_EX, LANES)
        first = 0.8 * state[1, :, :, columns].reshape(8 * N_EX, LANES) + 0.2 * grad
        second = 0.95 * state[2, :, :, columns].reshape(8 * N_EX, LANES) + 0.05 * grad * grad
        new = weight - 0.3 * (first / (jnp.sqrt(second) + 1e-08) + 0.1 * weight)
        fresh[part] = new.reshape(N_EX, 8, LANES)
        spread = lax.dot_general(
            pick[...],
            new.astype(jnp.bfloat16),
            (((0,), (0,)), ((), ())),
            preferred_element_type=jnp.float32,
        )
        hosted[part] = spread.astype(jnp.bfloat16).reshape(N_EX, 16, LANES)
        at = pl.ds(pl.multiple_of(HALF * my_half + LANES * part, LANES), LANES)

        def share_new(d, carry):
            j = lax.rem(me + d, N_EX)
            pltpu.make_async_remote_copy(
                src_ref=fresh.at[part, j],
                dst_ref=new_in.at[my_rows, at],
                send_sem=new_send,
                recv_sem=new_recv,
                device_id=(z, j),
                device_id_type=MESH,
            ).start()
            pltpu.make_async_remote_copy(
                src_ref=hosted.at[part, j],
                dst_ref=hosted_in.at[my_group, :, at],
                send_sem=hosted_send,
                recv_sem=hosted_recv,
                device_id=(z, j),
                device_id_type=MESH,
            ).start()
            return carry

        lax.fori_loop(1, N_EX, share_new, 0)
        pltpu.make_async_copy(fresh.at[part, me], new_in.at[my_rows, at], new_recv).start()
        pltpu.make_async_copy(
            hosted.at[part, me], hosted_in.at[my_group, :, at], hosted_recv
        ).start()

    pltpu.make_async_copy(state, state, state_recv).wait()
    for k in range(HOPS - LAG + LAST + 1, HOPS + 1):
        last_step(k)

    for part in range(LAST):
        pltpu.make_async_copy(slots_in.at[part], slots_in.at[part], sums_recv.at[part]).wait()
        value = expand(slots_in[part]).reshape(8 * SLOTS * N_EX, LANES)
        total = jnp.zeros((8 * N_EX, LANES), jnp.float32)
        for _ in range(2):
            piece = value.astype(jnp.bfloat16)
            value = value - piece.astype(jnp.float32)
            total = total + jnp.dot(pick[...], piece, preferred_element_type=jnp.float32)
        apply(part, total)

    last_copy(0, HOPS).wait_recv()
    up = last_arrived(0, HOPS)
    apply(
        LAST,
        jnp.concatenate([(last_own[g] + up[g]).reshape(BLOCK, LANES) for g in range(2)], axis=0),
    )

    pltpu.make_async_copy(new_in, new_in, new_recv).wait()
    pltpu.make_async_copy(hosted_in, hosted_in, hosted_recv).wait()

    for f, flow in enumerate(FLOWS):
        for k in range(1, flow[2] + 1):
            ring_copy(f, k).wait_send()
    for f, flow in enumerate(LAST_FLOWS):
        for k in range(1, flow[2] + 1):
            last_copy(f, k).wait_send()
    others = pl.ds(0, N_EX - 1)
    for sent, sem in (
        (level_in.at[others], level_send),
        (code_in.at[others], code_send),
        (state.at[:, others], state_send),
        (slots_in.at[:, others], sums_send),
        (fresh.at[:, others], new_send),
        (hosted.at[:, others], hosted_send),
    ):
        pltpu.make_async_copy(sent, sent, sem).wait()


def unpack(new_in, hosted_in, new_ref, weights_ref):
    new_ref[...] = new_in[...]
    for pair in range(8):
        both = [hosted_in[2 * pair + i].astype(jnp.float32) for i in range(2)]
        for s in range(SLOTS):
            block = jnp.concatenate([b[8 * s : 8 * s + 8] for b in both], axis=0)
            weights_ref[s, 16 * pair : 16 * pair + 16, :] = block.astype(jnp.bfloat16)


def body(x_rows, dy_rows, counts, host_table, owned, master, moment1, moment2):
    vmem = pl.BlockSpec(memory_space=pltpu.VMEM)
    hbm = pl.BlockSpec(memory_space=pltpu.HBM)
    dma = pltpu.SemaphoreType.DMA
    flows = len(FLOWS)
    new_pieces, hosted_pieces = pl.pallas_call(
        kernel,
        out_shape=(
            jax.ShapeDtypeStruct((BLOCK, FEATS), jnp.float32),
            jax.ShapeDtypeStruct((16, 16, FEATS), jnp.bfloat16),
        ),
        in_specs=[hbm] * 8,
        out_specs=(hbm, hbm),
        scratch_shapes=[
            pltpu.VMEM((SLOTS, CAP, WIDTH), jnp.bfloat16),
            pltpu.VMEM((SLOTS, CAP, FEATS), jnp.bfloat16),
            pltpu.SMEM((SLOTS,), jnp.int32),
            pltpu.SMEM((SLOTS, N_EX), jnp.int32),
            pltpu.SMEM((N_EX,), jnp.int32),
            pltpu.VMEM((3, BLOCK, FEATS), jnp.float32),
            pltpu.VMEM((PARTS, SLOTS, CAP, 2 * LANES), jnp.bfloat16),
            pltpu.VMEM((flows, HOPS, CHUNK, LANES), jnp.int16),
            pltpu.VMEM((flows, HOPS, CHUNK, LANES), jnp.int16),
            pltpu.VMEM((2, HOPS, LAST_CHUNK, LANES), jnp.int16),
            pltpu.VMEM((2, HOPS + 1, LAST_CHUNK, LANES), jnp.int16),
            pltpu.VMEM((2, 16, 8, LANES), jnp.float32),
            pltpu.VMEM((2 * HOPS, SLOTS, 2, 16, 8, LANES), jnp.float32),
            pltpu.VMEM((SLOTS, 2, 16, 8, LANES), jnp.float32),
            pltpu.VMEM((16, 2, 16, LANES), jnp.int16),
            pltpu.VMEM((N_EX, 16, LANES), jnp.int16),
            pltpu.VMEM((N_EX, 16, LANES), jnp.float32),
            pltpu.VMEM((16, 2, 2 * HOPS, 16, LANES), jnp.int16),
            pltpu.VMEM((N_EX, 2 * HOPS, 16, LANES), jnp.int16),
            pltpu.VMEM((8 * N_EX, 8 * SLOTS * N_EX), jnp.bfloat16),
            pltpu.VMEM((LAST, 16, 2, 16, LANES), jnp.int16),
            pltpu.VMEM((LAST, N_EX, 16, LANES), jnp.int16),
            pltpu.VMEM((3, N_EX, 8, HALF), jnp.float32),
            pltpu.VMEM((PARTS, N_EX, 8, LANES), jnp.float32),
            pltpu.VMEM((PARTS, N_EX, 16, LANES), jnp.bfloat16),
            dma((8,)),
            dma((flows, HOPS)),
            dma((flows, HOPS)),
            dma((2, HOPS)),
            dma((2, HOPS)),
            dma,
            dma,
            dma,
            dma((HOPS,)),
            dma,
            dma,
            dma,
            dma((LAST,)),
            dma,
            dma,
            dma,
            dma,
        ],
        compiler_params=pltpu.CompilerParams(
            collective_id=0, has_side_effects=True, vmem_limit_bytes=62 * 1024 * 1024
        ),
    )(
        x_rows[0], dy_rows[0], counts.reshape(SLOTS), host_table.T, owned,
        master[0], moment1[0], moment2[0],
    )
    new_master, host_weights = pl.pallas_call(
        unpack,
        out_shape=(
            jax.ShapeDtypeStruct((BLOCK, FEATS), jnp.float32),
            jax.ShapeDtypeStruct((SLOTS, BLOCK, FEATS), jnp.bfloat16),
        ),
        in_specs=[vmem, vmem],
        out_specs=(vmem, vmem),
        compiler_params=pltpu.CompilerParams(vmem_limit_bytes=62 * 1024 * 1024),
    )(new_pieces, hosted_pieces)
    return (new_master[None], host_weights[None])


def solution(mesh):
    in_specs = (
        P("expert", None, "dp", None),
        P("expert", None, "dp", None),
        P("expert", None, "dp"),
        P(),
        P(),
        P("expert", "dp", None),
        P("expert", "dp", None),
        P("expert", "dp", None),
    )
    out_specs = (P("expert", "dp", None), P("expert", None, "dp", None))
    return jax.shard_map(body, mesh=mesh, in_specs=in_specs, out_specs=out_specs, check_vma=False)
```
